512 devices in a mesh: sec: 4 (over x_hi, core), gx: 16 (over x_lo, z), gy: 8 (over y).
Axes of the slice: x: 4 (x_hi: 2, x_lo: 2; x = x_hi * 2 + x_lo), y: 8, z: 8, core: 2. Of those that a mesh axis runs over, the one named last changes fastest.
Arguments:
- profile: bfloat16 [4, 128, 512, 1024], P('sec', None, 'gx', 'gy'), may hold values from -6 to 6
- surface: float32 [4, 512, 1024], P('sec', 'gx', 'gy'), may hold values from -6 to 6
- diffusion: float32 [4, 512, 1024], P('sec', 'gx', 'gy'), may hold values from 0.05 to 0.24
- sea_mask: int32 [4, 512, 1024], P('sec', 'gx', 'gy'), may hold values 0 or 1
- convective: int32 [4, 512, 1024], P('sec', 'gx', 'gy'), may hold values from 0 to 1, as said below
- mixing: bfloat16 [4, 2, 128, 128], P('sec'), may hold values from -0.5 to 0.5
- remap_weights: bfloat16 [4, 16, 8, 32, 2, 128, 128], P('sec', 'gx', 'gy'), may hold values from -0.375 to 0.375
- sources: int32 [4, 16, 8, 32, 2], P('sec', 'gx', 'gy'), may hold values from 0 to 127, as said below
- send_lists: int32 [4, 16, 8, 64, 2], P('sec', 'gx', 'gy'), may hold values from 0 to 31
Outputs:
- column_state: bfloat16 [4, 128, 512, 1024], P('sec', None, 'gx', 'gy')
- surface_state: float32 [4, 512, 1024], P('sec', 'gx', 'gy')
The draws below stay inside these ranges and needn't reach their ends.
Inputs may be any that keep to these rules, and one draw needn't show every extreme that they name: sources[s, i, j, a, k] = e * 2 + c names slot c from sender e = s2 * 16 + i2 at the same j; for s below 3 the sender has s2 = 3, for s = 3 it has s2 below 3. `convective`: each device holds 64 to 1024 columns with 1, and some device exactly 1024.
All inputs are finite; a program needn't handle non-finite values. No bound on the sum of `sea_mask` on one device may be relied on, other than what follows from the above.
Results may differ from the reference program's by a relative error of at most 0.0074.
Values may be sent and summed in bfloat16 or wider, within the bound.
No kernel may reach another device: no remote copies, remote signals or barrier semaphores. Data moves between devices by JAX's collectives and lax.ppermute only.
A program may use at most 64 MiB of HBM per device.

```python
import jax
import jax.numpy as jnp
from jax import lax

LEV = 128
TILE = 128
K = 2
CAP = 2
STEPS = 2
PHYS = 4
PASSES = 4
NX = 32
NY = 128
AT = 32
G = 64
NXT = 512
NYT = 1024
CMAX = 1024
CMIN = 64
N_SEC = 4
N_GX = 16
N_GY = 8


def draw_sources(key, part):
    key = jax.random.fold_in(key, 23)
    first, second, third = jax.random.split(key, 3)
    shape = (N_SEC, N_GX, N_GY, AT, K)
    section = jnp.arange(N_SEC, dtype=jnp.int32).reshape(N_SEC, 1, 1, 1, 1)
    from_air = jax.random.randint(first, shape, 0, (N_SEC - 1) * N_GX, dtype=jnp.int32)
    from_ocean = (N_SEC - 1) * N_GX + jax.random.randint(second, shape, 0, N_GX, dtype=jnp.int32)
    sender = jnp.where(section == N_SEC - 1, from_air, from_ocean)
    slot_index = jax.random.randint(third, shape, 0, CAP, dtype=jnp.int32)
    return sender * CAP + slot_index


def draw_convective(key, part):
    key = jax.random.fold_in(key, 11)
    first, second, third = jax.random.split(key, 3)
    devices = N_SEC * N_GX * N_GY
    cell_count = NX * NY
    counts = jax.random.randint(first, (devices,), CMIN, CMAX + 1, dtype=jnp.int32)
    fullest = jax.random.randint(second, (), 0, devices, dtype=jnp.int32)
    counts = jnp.where(jnp.arange(devices, dtype=jnp.int32) == fullest, CMAX, counts)
    ranks = jax.vmap(lambda single: jax.random.permutation(single, cell_count))(jax.random.split(third, devices))
    marked = (ranks.astype(jnp.int32) < counts[:, None]).astype(jnp.int32)
    shaped = marked.reshape(N_SEC, N_GX, N_GY, NX, NY).transpose(0, 1, 3, 2, 4)
    return shaped.reshape(N_SEC, NX * N_GX, NY * N_GY)


def touch_ends(array, key, low, largest):
    dims = array.shape
    place = [jax.random.randint(jax.random.fold_in(key, axis), (), 0, dims[axis]) for axis in range(len(dims))]
    array = array.at[tuple(place)].set(low)
    longest = dims.index(max(dims))
    place[longest] = (place[longest] + 1) % dims[longest]
    return array.at[tuple(place)].set(largest)


def block_levels(key, dims, cuts, smallest, high):
    factor_of, own = 1.0, jax.random.fold_in(key, 6)
    for position, shards_of in cuts:
        draws = jnp.exp(jax.random.uniform(jax.random.fold_in(own, position), (shards_of,), jnp.float32, smallest / len(cuts), high / len(cuts)))
        factor_of = factor_of * jnp.repeat(draws, dims[position] // shards_of).reshape([-1 if axis == position else 1 for axis in range(len(dims))])
    return factor_of


def gaussian(own_key, extent, scale, bound, cuts=(), kind=jnp.bfloat16):
    array = jax.random.normal(own_key, extent, jnp.float32) * scale
    if len(cuts) > 0:
        array = block_levels(own_key, extent, cuts, -0.22, 0.18) * array
    return jnp.clip(array, min=-bound, max=bound).astype(kind)


def setup_inputs(seed: int = 0) -> dict:
    key_of = jax.random.split(jax.random.key(seed), 10)
    profile = gaussian(key_of[0], (N_SEC, LEV, NXT, NYT), 1.0, 6.0, ((0, 4), (2, 16), (3, 8)))
    surface = gaussian(key_of[1], (N_SEC, NXT, NYT), 1.0, 6.0, ((0, 4), (1, 16), (2, 8)), jnp.float32)
    diffusion = jnp.clip(0.05 + 0.19 * jax.random.uniform(key_of[2], (N_SEC, NXT, NYT), jnp.float32) ** block_levels(key_of[2], (N_SEC, NXT, NYT), ((0, 4), (1, 16), (2, 8)), -0.2, 0.2), 0.05, 0.24)
    sea_mask = touch_ends((jax.random.randint(key_of[3], (N_SEC, NXT, NYT), 0, 4) < 3).astype(jnp.int32), jax.random.fold_in(key_of[3], 1), 0, 1)
    convective = draw_convective(jax.random.fold_in(key_of[9], 71), 0)
    mixing = gaussian(key_of[5], (N_SEC, 2, LEV, LEV), LEV ** -0.5, 0.5, ((0, 4),))
    remap_weights = gaussian(key_of[6], (N_SEC, N_GX, N_GY, AT, K, TILE, TILE), (K * TILE) ** -0.5, 0.375, ((0, 4), (1, 16), (2, 8)))
    sources = draw_sources(jax.random.fold_in(key_of[9], 71), 0)
    send_lists = touch_ends(jax.random.randint(key_of[8], (N_SEC, N_GX, N_GY, G, CAP), 0, AT), jax.random.fold_in(key_of[8], 1), 0, AT - 1).astype(jnp.int32)
    return dict(profile=profile, surface=surface, diffusion=diffusion, sea_mask=sea_mask, convective=convective, mixing=mixing, remap_weights=remap_weights, sources=sources, send_lists=send_lists)


def to_tiles(field):
    shaped = field.reshape(N_SEC, N_GX, NX, N_GY, NY).transpose(0, 1, 3, 2, 4)
    return shaped.reshape(N_SEC, N_GX, N_GY, AT, TILE)


def from_tiles(tiled):
    shaped = tiled.reshape(N_SEC, N_GX, N_GY, NX, NY).transpose(0, 1, 3, 2, 4)
    return shaped.reshape(N_SEC, NX * N_GX, NY * N_GY)


def take_rows(table, index):
    return table[index]


def remap_column(packed):
    buffer, chosen, weights = packed
    picked = jax.vmap(take_rows)(buffer, chosen)
    return jnp.einsum("gakij,gakj->gai", weights.astype(jnp.float32), picked.astype(jnp.float32))


def remap_all(tiles, remap_weights, sources, send_lists):
    senders = N_SEC * N_GX
    by_column = tiles.transpose(2, 0, 1, 3, 4).reshape(N_GY, senders, AT, TILE)
    lists = send_lists.transpose(2, 0, 1, 3, 4).reshape(N_GY, senders, senders, CAP)
    outgoing = jax.vmap(jax.vmap(take_rows))(by_column, lists)
    buffer = outgoing.transpose(0, 2, 1, 3, 4).reshape(N_GY, senders, senders * CAP, TILE)
    chosen = sources.transpose(2, 0, 1, 3, 4).reshape(N_GY, senders, AT, K)
    weights = remap_weights.transpose(2, 0, 1, 3, 4, 5, 6).reshape(N_GY, senders, AT, K, TILE, TILE)
    imported = lax.map(remap_column, (buffer, chosen, weights))
    return imported.reshape(N_GY, N_SEC, N_GX, AT, TILE).transpose(1, 2, 0, 3, 4)


def smooth(height, diffusion, sea_float, forcing):
    padded = jnp.pad(height, ((0, 0), (1, 1), (1, 1)))
    beside_all = padded[:, 2:, 1:-1] + padded[:, :-2, 1:-1]
    beside_all = beside_all + padded[:, 1:-1, 2:] + padded[:, 1:-1, :-2]
    return sea_float * (height + diffusion * (beside_all - 4.0 * height) + forcing)


def physics_section(packed):
    column, branch, matrices = packed
    flat = column.reshape(LEV, -1)
    chosen = branch.reshape(-1) == 1
    for substep in range(PHYS):
        plain_mix = jnp.dot(matrices[0], flat, preferred_element_type=jnp.float32)
        deep_mix = jnp.dot(matrices[1], flat, preferred_element_type=jnp.float32)
        mixed = jnp.where(chosen, deep_mix, plain_mix)
        flat = (0.5 * flat.astype(jnp.float32) + jnp.tanh(mixed)).astype(jnp.bfloat16)
    return flat.reshape(column.shape)


def reference(profile, surface, diffusion, sea_mask, convective, mixing, remap_weights, sources, send_lists):
    sea_float = sea_mask.astype(jnp.float32)
    column_state = profile
    surface_state = surface
    last = N_SEC - 1
    for coupled in range(STEPS):
        lowest = column_state[:, 0]
        imported = from_tiles(remap_all(to_tiles(lowest), remap_weights, sources, send_lists))
        flux = sea_float * (imported - lowest.astype(jnp.float32))
        forcing = flux / PASSES
        ocean = surface_state[last:]
        for sweep in range(PASSES):
            ocean = smooth(ocean, diffusion[last:], sea_float[last:], forcing[last:])
        surface_state = jnp.concatenate([surface_state[:last], ocean], axis=0)
        bottom = (lowest.astype(jnp.float32) + flux).astype(jnp.bfloat16)
        forced = column_state.at[:, 0].set(bottom)
        atmosphere = lax.map(physics_section, (forced[:last], convective[:last], mixing[:last]))
        column_state = jnp.concatenate([atmosphere, column_state[last:]], axis=0)
    return column_state, surface_state
```

```python
import jax
import jax.numpy as jnp
from jax import lax
from jax.sharding import PartitionSpec as P

STEPS = 2
PHYS = 4
PASSES = 4
HALO = 4


def body(
    profile, surface, diffusion, sea_mask, convective, mixing, remap_weights, sources, send_lists
):
    levels = profile.shape[1]
    grid_rows = profile.shape[2]
    grid_cols = profile.shape[3]
    cell_count = grid_rows * grid_cols
    tile_size = remap_weights.shape[-1]
    column_state = profile.reshape(levels, cell_count)
    start_surface = surface.reshape(grid_rows, grid_cols)
    coefficient = diffusion.reshape(grid_rows, grid_cols)
    sea_float = sea_mask.reshape(grid_rows, grid_cols).astype(jnp.float32)
    deep_flags = convective.reshape(cell_count) == 1
    matrices = mixing.reshape(2, levels, levels)
    weights = remap_weights.reshape(remap_weights.shape[3:])
    wanted = sources.reshape(sources.shape[3:])
    lists = send_lists.reshape(send_lists.shape[3:])
    senders, slot_count = lists.shape
    sec_count = lax.axis_size("sec")
    gx_count = lax.axis_size("gx")
    gy_count = lax.axis_size("gy")
    ocean_side = lax.axis_index("sec") == sec_count - 1
    base_x = (sec_count - 1) * gx_count
    base_y = (sec_count - 1) * gy_count

    def advance(state):
        for substep in range(PHYS):
            plain_mix = jnp.dot(matrices[0], state, preferred_element_type=jnp.float32)
            deep_mix = jnp.dot(matrices[1], state, preferred_element_type=jnp.float32)
            mixed = jnp.where(deep_flags, deep_mix, plain_mix)
            state = (0.5 * state.astype(jnp.float32) + jnp.tanh(mixed)).astype(jnp.bfloat16)
        return state

    def exchange(lowest):
        tiles = lowest.reshape(cell_count // tile_size, tile_size)
        chosen = tiles[lists]
        return lax.all_to_all(chosen, ("sec", "gx"), 0, 0, tiled=True)

    def remap(received):
        picked = received.reshape(senders * slot_count, tile_size)[wanted]
        return jnp.einsum("akij,akj->ai", weights, picked, preferred_element_type=jnp.float32)

    def widen(fields):
        up = [(base_x + i, base_x + i + 1) for i in range(gx_count - 1)]
        down = [(t, s) for s, t in up]
        before = lax.ppermute(fields[:, -HALO:, :], ("sec", "gx"), up)
        after = lax.ppermute(fields[:, :HALO, :], ("sec", "gx"), down)
        fields = jnp.concatenate([before, fields, after], axis=1)
        up = [(base_y + i, base_y + i + 1) for i in range(gy_count - 1)]
        down = [(t, s) for s, t in up]
        before = lax.ppermute(fields[:, :, -HALO:], ("sec", "gy"), up)
        after = lax.ppermute(fields[:, :, :HALO], ("sec", "gy"), down)
        return jnp.concatenate([before, fields, after], axis=2)

    def passes(height, forcing, coef, sea):
        for sweep in range(PASSES):
            around = height[2:, 1:-1] + height[:-2, 1:-1]
            around = around + height[1:-1, 2:] + height[1:-1, :-2]
            inner = height[1:-1, 1:-1]
            cut = sweep + 1
            rows = slice(cut, coef.shape[0] - cut)
            cols = slice(cut, coef.shape[1] - cut)
            height = sea[rows, cols] * (
                inner + coef[rows, cols] * (around - 4.0 * inner) + forcing[rows, cols]
            )
        return height

    still = widen(jnp.stack([start_surface, coefficient, sea_float]))
    lowest = column_state[0]
    imported = remap(exchange(lowest))
    flux = sea_float * (imported - lowest.reshape(grid_rows, grid_cols).astype(jnp.float32))

    def bottom_of(lowest, flux):
        return (lowest.astype(jnp.float32) + flux.reshape(cell_count)).astype(jnp.bfloat16)

    def unchanged(state, bottom):
        return state

    def forced_advance(state, bottom):
        return advance(state.at[0].set(bottom))

    first = lax.cond(ocean_side, unchanged, forced_advance, column_state, bottom_of(lowest, flux))
    lowest_1 = first[0]
    received_1 = exchange(lowest_1)

    forcing = widen((flux / PASSES)[None])[0]
    height = passes(still[0], forcing, still[1], still[2])

    flux_air = sea_float * (imported - lowest_1.reshape(grid_rows, grid_cols).astype(jnp.float32))
    column_state = lax.cond(ocean_side, unchanged, forced_advance, first, bottom_of(lowest_1, flux_air))

    imported_1 = remap(received_1)
    flux_1 = sea_float * (imported_1 - lowest_1.reshape(grid_rows, grid_cols).astype(jnp.float32))
    both = widen(jnp.stack([height, flux_1 / PASSES]))
    height = passes(both[0], both[1], still[1], still[2])
    surface_out = jnp.where(ocean_side, height, start_surface)
    return (column_state.reshape(profile.shape), surface_out.reshape(surface.shape))


def solution(mesh):
    return jax.shard_map(
        body,
        mesh=mesh,
        in_specs=(
            P("sec", None, "gx", "gy"),
            P("sec", "gx", "gy"),
            P("sec", "gx", "gy"),
            P("sec", "gx", "gy"),
            P("sec", "gx", "gy"),
            P("sec", None, None, None),
            P("sec", "gx", "gy", None, None, None, None),
            P("sec", "gx", "gy", None, None),
            P("sec", "gx", "gy", None, None),
        ),
        out_specs=(P("sec", None, "gx", "gy"), P("sec", "gx", "gy")),
        check_vma=False,
    )
```

```python
import functools

import jax
import jax.numpy as jnp
from jax import lax
from jax.experimental import pallas as pl
from jax.experimental.pallas import tpu as pltpu
from jax.sharding import PartitionSpec as P

PHYS = 4
PASSES = 4
HALO = 8
NEAR = 3
PLANES = 5
WIDTH = 2048
MESSAGE = 6
bf16 = jnp.bfloat16
f32 = jnp.float32
VMEM_LIMIT = 24 * 1024 * 1024


def call(kernel, outs, name, in_specs=None, scratch=(), flops=0):
    more = {} if in_specs is None else {"in_specs": in_specs, "grid": (1,)}
    return pl.pallas_call(
        kernel,
        out_shape=[jax.ShapeDtypeStruct(shape, kind) for shape, kind in outs],
        scratch_shapes=list(scratch),
        name=name,
        cost_estimate=pl.CostEstimate(flops=flops, bytes_accessed=1 << 20, transcendentals=0),
        compiler_params=pltpu.CompilerParams(vmem_limit_bytes=VMEM_LIMIT),
        **more,
    )


def whole():
    return pl.BlockSpec(memory_space=pltpu.VMEM)


def is_ocean():
    return lax.axis_index("sec") == lax.axis_size("sec") - 1


def iota(shape, dim):
    return lax.broadcasted_iota(jnp.int32, shape, dim)


def one_hot(flags):
    return jnp.where(flags, 1.0, 0.0).astype(bf16)


def take(hot, rows):
    return jnp.dot(hot, rows, preferred_element_type=f32).astype(bf16)


def listed(tiles, lists):
    place = iota((lists.shape[0], tiles.shape[0]), 1)
    return jnp.concatenate(
        [take(one_hot(lists[:, c : c + 1] == place), tiles) for c in range(lists.shape[1])], axis=0
    )


def select_kernel(level_ref, lists_ref, out_ref, lowest_ref):
    lists = lists_ref[...]
    senders = lists.shape[0]
    tiles = level_ref[0, 0]
    lowest_ref[...] = tiles.astype(f32)
    chosen = listed(tiles, lists)
    row = iota((out_ref.shape[0], chosen.shape[0]), 0)
    col = iota((out_ref.shape[0], chosen.shape[0]), 1)
    out_ref[...] = take(one_hot(col == (row & 1) * senders + (row >> 1)), chosen)


def edges_kernel(*refs):
    surface, diffusion, sea, lowest, sources = refs[:5]
    weights = refs[5 : 5 + 2 * NEAR]
    to_next, to_prev = refs[-2:]
    rows = surface.shape[0]
    for out, first, blocks in ((to_prev, 0, weights[:NEAR]), (to_next, rows - HALO, weights[NEAR:])):
        part = slice(first, first + HALO)
        out[0:HALO] = surface[part]
        out[HALO : 2 * HALO] = diffusion[part]
        out[2 * HALO : 3 * HALO] = sea[part].astype(f32)
        out[3 * HALO : 4 * HALO] = lowest[part]
        out[4 * HALO : 5 * HALO] = jnp.zeros((HALO, out.shape[1]), f32)
        out[4 * HALO : 5 * HALO, 0:2] = sources[part].astype(f32)
        base = PLANES * HALO
        for block in blocks:
            for k in range(2):
                size = block.shape[2]
                out[base : base + size] = block[0, k].astype(f32)
                base += size


def import_row(pick_ref, a, first, second):
    row = pick_ref[a : a + 1, :].astype(bf16)
    block = jnp.concatenate([first, second], axis=1)
    return lax.dot_general(row, block, (((1,), (1,)), ((), ())), preferred_element_type=f32)


def substep(x, flag, mix):
    deep = x * flag
    both = jnp.concatenate([x - deep, deep], axis=0)
    mixed = jnp.dot(mix, both, preferred_element_type=f32)
    return (0.5 * x.astype(f32) + jnp.tanh(mixed)).astype(bf16)


def with_bottom(x, bottom):
    top = x[0:16].astype(f32)
    top = jnp.where(iota(top.shape, 0) == 0, bottom, top).astype(bf16)
    return jnp.concatenate([top, x[16:]], axis=0)


def flat_rows(grid, first, count):
    return jnp.concatenate([grid[first + r : first + r + 1] for r in range(count)], axis=1)


def first_kernel(
    received, sources, weights, lowest_ref, sea, x_ref, flag_ref, mixing, lists_ref,
    state, message, low, carry, pick, low_f,
):
    src = sources[...]
    rows = src.shape[0]
    place = iota((rows, received.shape[0]), 1)
    tile = received.shape[1]
    for k in range(2):
        hot = one_hot(src[:, k : k + 1] == place)
        pick[:, k * tile : (k + 1) * tile] = jnp.dot(hot, received[...], preferred_element_type=f32)
    for a in range(rows):
        carry[a : a + 1, :] = import_row(pick, a, weights[a, 0], weights[a, 1])
    lowest = lowest_ref[...]
    flux = sea[...].astype(f32) * (carry[...] - lowest)

    @pl.when(is_ocean())
    def _():
        carry[...] = flux * (1.0 / PASSES)
        message[...] = jnp.zeros(message.shape, bf16)

    @pl.when(jnp.logical_not(is_ocean()))
    def _():
        mix = jnp.concatenate([mixing[0], mixing[1]], axis=1)
        bottom = (lowest + flux).astype(bf16).astype(f32)
        per = WIDTH // tile
        for c in range(x_ref.shape[1] // WIDTH):
            cols = slice(c * WIDTH, (c + 1) * WIDTH)
            flag = flag_ref[:, cols]
            x = with_bottom(x_ref[:, cols], flat_rows(bottom, c * per, per))
            for _ in range(PHYS - 1):
                x = substep(x, flag, mix)
            state[:, cols] = x
            deep = x * flag
            both = jnp.concatenate([x - deep, deep], axis=0)
            mixed = jnp.dot(mix[0:16], both, preferred_element_type=f32)
            last = 0.5 * x[0:16].astype(f32) + jnp.tanh(mixed)
            for r in range(per):
                low_f[c * per + r : c * per + r + 1, :] = last[0:1, r * tile : (r + 1) * tile]
        tiles = low_f[...].astype(bf16)
        low[...] = tiles
        lists = lists_ref[...]
        senders = lists.shape[0]
        chosen = listed(tiles, lists)
        row = iota((message.shape[0], chosen.shape[0]), 0)
        col = iota((message.shape[0], chosen.shape[0]), 1)
        target = (row * 10923) >> 16
        m = row - MESSAGE * target
        message[...] = take(one_hot(col == (m & 1) * senders + target - 1 + (m >> 1)), chosen)


def second_kernel(state, low, carry, sea, x_ref, flag_ref, mixing, out, to_next, to_prev):
    @pl.when(is_ocean())
    def _():
        rows = carry.shape[0]
        to_prev[...] = carry[0:HALO]
        to_next[...] = carry[rows - HALO : rows]
        out[...] = x_ref[...]

    @pl.when(jnp.logical_not(is_ocean()))
    def _():
        mix = jnp.concatenate([mixing[0], mixing[1]], axis=1)
        lowest = low[...].astype(f32)
        flux = sea[...].astype(f32) * (carry[...] - lowest)
        bottom = (lowest + flux).astype(bf16).astype(f32)
        per = WIDTH // low.shape[1]
        for c in range(x_ref.shape[1] // WIDTH):
            cols = slice(c * WIDTH, (c + 1) * WIDTH)
            flag = flag_ref[:, cols]
            x = substep(state[:, cols], flag, mix)
            x = with_bottom(x, flat_rows(bottom, c * per, per))
            for _ in range(PHYS):
                x = substep(x, flag, mix)
            out[:, cols] = x


def third_kernel(
    received, sources, weights, lowest_ref, sea, surface, diffusion, forcing, still_above, still_below,
    forcing_above, forcing_below, wide, to_right, to_left, pick, imported,
):
    @pl.when(is_ocean())
    def _():
        rows, tile = surface.shape

        def plane(own, p):
            part = slice(p * HALO, (p + 1) * HALO)
            return jnp.concatenate([own, still_below[part], still_above[part]], axis=0)

        part = slice(4 * HALO, 5 * HALO)
        src = jnp.concatenate(
            [sources[...], still_below[part, 0:2].astype(jnp.int32), still_above[part, 0:2].astype(jnp.int32)],
            axis=0,
        )
        total = src.shape[0]
        row = iota((total, 1), 0)
        offset = jnp.where(row < rows, 2, jnp.where(row < rows + HALO, 4, 0))
        place = iota((total, received.shape[0]), 1)
        for k in range(2):
            q = src[:, k : k + 1]
            hot = one_hot((q >> 1) * MESSAGE + (q & 1) + offset == place)
            pick[:, k * tile : (k + 1) * tile] = jnp.dot(hot, received[...], preferred_element_type=f32)
        imported[...] = jnp.zeros(imported.shape, f32)
        for a in range(rows):
            imported[a : a + 1, :] = import_row(pick, a, weights[a, 0], weights[a, 1])
        for still, first in ((still_below, rows), (still_above, total - NEAR)):
            for n in range(NEAR):
                base = PLANES * HALO + 2 * n * tile
                blocks = [still[base + k * tile : base + (k + 1) * tile, :].astype(bf16) for k in range(2)]
                a = first + n
                imported[a : a + 1, :] = import_row(pick, a, blocks[0], blocks[1])
        sea_all = plane(sea[...].astype(f32), 2)
        lowest = plane(lowest_ref[...], 3)
        planes = [
            jnp.concatenate([forcing[...], forcing_below[...], forcing_above[...]], axis=0),
            sea_all * (imported[...] - lowest) * (1.0 / PASSES),
            plane(surface[...], 0),
            plane(diffusion[...], 1),
            sea_all,
        ]
        group = iota((total, tile), 1) >> 3
        right = planes[0]
        left = planes[0]
        for p, values in enumerate(planes):
            wide[p] = values
            if p:
                right = jnp.where(group == tile // HALO - 1 - p, pltpu.roll(values, tile - HALO * p, 1), right)
                left = jnp.where(group == p, pltpu.roll(values, HALO * p, 1), left)
        to_right[...] = right
        to_left[...] = left


def fourth_kernel(wide, from_left, from_right, surface, out):
    @pl.when(jnp.logical_not(is_ocean()))
    def _():
        out[...] = surface[...]

    @pl.when(is_ocean())
    def _():
        rows, tile = surface.shape
        total = wide.shape[1]
        group = iota((total, tile), 1) >> 3
        fields = []
        for p in range(PLANES):
            right, left = from_right[...], from_left[...]
            if p:
                right = pltpu.roll(right, tile - HALO * p, 1)
                left = pltpu.roll(left, HALO * p, 1)
            beside = jnp.where(group == 0, right, jnp.where(group == tile // HALO - 1, left, 0.0))
            fields.append(jnp.concatenate([wide[p], beside], axis=1))
        first, second, height, coefficient, sea = fields
        for forcing in (first, second):
            for sweep in range(PASSES):
                around = pltpu.roll(height, total - 1, 0) + pltpu.roll(height, 1, 0)
                around = around + pltpu.roll(height, 2 * tile - 1, 1) + pltpu.roll(height, 1, 1)
                height = sea * (height + coefficient * (around - 4.0 * height) + forcing)
        out[...] = height[0:rows, 0:tile]


def body(
    profile, surface, diffusion, sea_mask, convective, mixing, remap_weights, sources, send_lists
):
    levels, rows, tile = profile.shape[1:]
    cells = rows * tile
    surface_2d = surface.reshape(rows, tile)
    coefficient = diffusion.reshape(rows, tile)
    sea = sea_mask.reshape(rows, tile)
    matrices = mixing.reshape(2, levels, levels)
    weights = remap_weights.reshape(remap_weights.shape[3:])
    wanted = sources.reshape(sources.shape[3:])
    lists = send_lists.reshape(send_lists.shape[3:])
    senders, slots = lists.shape
    secs = lax.axis_size("sec")
    gx = lax.axis_size("gx")
    gy = lax.axis_size("gy")
    total = rows + 2 * HALO
    level = pl.BlockSpec((1, 1, rows, tile), lambda i: (0, 0, 0, 0))

    def along(axis, count, to_next, to_prev):
        base = (secs - 1) * count
        up = [(base + i, base + i + 1) for i in range(count - 1)]
        down = [(t, s) for s, t in up]
        return lax.ppermute(to_next, ("sec", axis), up), lax.ppermute(to_prev, ("sec", axis), down)

    chosen, lowest = call(
        select_kernel,
        [((senders * slots, tile), bf16), ((rows, tile), f32)],
        "select_tiles",
        [level, whole()],
    )(profile, lists)
    received = lax.all_to_all(chosen.reshape(senders, slots, tile), ("sec", "gx"), 0, 0, tiled=True)

    def near(a):
        return pl.BlockSpec((1, 2, tile, tile), lambda i: (a, 0, 0, 0))

    nears = [near(a) for a in (*range(NEAR), *range(rows - NEAR, rows))]
    height = PLANES * HALO + NEAR * 2 * tile
    still_next, still_prev = call(
        edges_kernel,
        [((height, tile), f32)] * 2,
        "edge_rows",
        [whole()] * 5 + nears,
    )(surface_2d, coefficient, sea, lowest, wanted, *[weights] * (2 * NEAR))
    still_above, still_below = along("gx", gx, still_next, still_prev)

    columns = profile.reshape(levels, cells)
    flag = convective.reshape(1, cells).astype(bf16)
    state, message, low, carry = call(
        first_kernel,
        [
            ((levels, cells), bf16),
            ((senders * MESSAGE, tile), bf16),
            ((rows, tile), bf16),
            ((rows, tile), f32),
        ],
        "first_step",
        scratch=[pltpu.VMEM((rows, 2 * tile), f32), pltpu.VMEM((rows, tile), f32)],
        flops=1 << 30,
    )(
        received.reshape(senders * slots, tile), wanted, weights, lowest, sea, columns, flag,
        matrices, lists,
    )
    again = lax.all_to_all(
        message.reshape(senders * MESSAGE // 2, 2, tile), ("sec", "gx"), 0, 0, tiled=True
    )
    final, forcing_next, forcing_prev = call(
        second_kernel,
        [((levels, cells), bf16), ((HALO, tile), f32), ((HALO, tile), f32)],
        "second_step",
        flops=1 << 31,
    )(state, low, carry, sea, columns, flag, matrices)
    forcing_above, forcing_below = along("gx", gx, forcing_next, forcing_prev)

    wide, to_right, to_left = call(
        third_kernel,
        [((PLANES, total, tile), f32), ((total, tile), f32), ((total, tile), f32)],
        "second_import",
        scratch=[pltpu.VMEM((total, 2 * tile), f32), pltpu.VMEM((total, tile), f32)],
    )(
        again.reshape(senders * MESSAGE, tile), wanted, weights, lowest, sea, surface_2d,
        coefficient, carry, still_above, still_below, forcing_above, forcing_below,
    )
    from_left, from_right = along("gy", gy, to_right, to_left)
    (surface_out,) = call(fourth_kernel, [((rows, tile), f32)], "passes")(
        wide, from_left, from_right, surface_2d
    )
    return (final.reshape(profile.shape), surface_out.reshape(surface.shape))


def solution(mesh):
    return jax.shard_map(
        body,
        mesh=mesh,
        in_specs=(
            P("sec", None, "gx", "gy"),
            P("sec", "gx", "gy"),
            P("sec", "gx", "gy"),
            P("sec", "gx", "gy"),
            P("sec", "gx", "gy"),
            P("sec", None, None, None),
            P("sec", "gx", "gy", None, None, None, None),
            P("sec", "gx", "gy", None, None),
            P("sec", "gx", "gy", None, None),
        ),
        out_specs=(P("sec", None, "gx", "gy"), P("sec", "gx", "gy")),
        check_vma=False,
    )
```

```python
import functools

import jax
import jax.numpy as jnp
from jax import lax
from jax.experimental import pallas as pl
from jax.experimental.pallas import tpu as pltpu
from jax.sharding import PartitionSpec as P

PHYS = 4
PASSES = 4
HALO = 8
NEAR = 3
PLANES = 5
WIDTH = 2048
MESSAGE = 6
bf16 = jnp.bfloat16
f32 = jnp.float32
HBM = pltpu.HBM
VMEM = pltpu.VMEM
VMEM_LIMIT = 16 * 1024 * 1024


def call(kernel, name, operands, outs, scratch=(), flops=0):
    values, specs = [], []
    for operand in operands:
        value, place = operand if isinstance(operand, tuple) else (operand, None)
        if place is not None:
            value = pltpu.with_memory_space_constraint(value, place)
        values.append(value)
        specs.append(pl.BlockSpec(memory_space=HBM if place is HBM else VMEM))
    shapes = [
        out[2](out[0], out[1]) if len(out) > 2 else jax.ShapeDtypeStruct(out[0], out[1]) for out in outs
    ]
    return pl.pallas_call(
        kernel,
        out_shape=shapes,
        in_specs=specs,
        out_specs=[pl.BlockSpec(memory_space=out[2] if len(out) > 2 else VMEM) for out in outs],
        scratch_shapes=list(scratch),
        name=name,
        cost_estimate=pl.CostEstimate(flops=flops, bytes_accessed=1 << 20, transcendentals=0),
        compiler_params=pltpu.CompilerParams(vmem_limit_bytes=VMEM_LIMIT),
    )(*values)


def fetch(sems, *pairs):
    copies = [pltpu.make_async_copy(source, target, sems.at[n]) for n, (source, target) in enumerate(pairs)]
    for copy in copies:
        copy.start()
    return copies


def is_ocean():
    return lax.axis_index("sec") == lax.axis_size("sec") - 1


def is_even(axis):
    return lax.rem(lax.axis_index(axis), 2) == 0


def iota(shape, dim):
    return lax.broadcasted_iota(jnp.int32, shape, dim)


def one_hot(flags):
    return jnp.where(flags, 1.0, 0.0).astype(bf16)


def spread(rows, column, odd):
    hot = one_hot(iota((column.shape[0], rows.shape[1]), 1) == column)
    values = rows.astype(f32).astype(bf16)
    both = lax.dot_general(hot, values, (((1,), (1,)), ((), ())), preferred_element_type=f32)
    return jnp.where(odd == 1, both[:, 1:2], both[:, 0:1]).astype(jnp.int32)


def upright(rows, first=0, count=None):
    count = rows.shape[1] if count is None else count
    unit = one_hot(iota((count, rows.shape[1]), 0) + first == iota((count, rows.shape[1]), 1))
    values = rows.astype(f32).astype(bf16)
    turned = lax.dot_general(unit, values, (((1,), (1,)), ((), ())), preferred_element_type=f32)
    return turned.astype(jnp.int32)


def select_kernel(profile, lists_ref, out_ref, tiles_v, lists_v, sems):
    copies = fetch(sems, (lists_ref, lists_v), (profile.at[0, 0], tiles_v))
    row = iota((out_ref.shape[0], 1), 0)
    copies[0].wait()
    tile = spread(lists_v[...], row >> 1, row & 1)
    hot = one_hot(iota((out_ref.shape[0], tiles_v.shape[0]), 1) == tile)
    copies[1].wait()
    out_ref[...] = jnp.dot(hot, tiles_v[...], preferred_element_type=f32).astype(bf16)


def edges_kernel(
    surface, diffusion, sea, profile, sources, weights, to_a, to_b,
    surface_v, diffusion_v, sea_v, level_v, sources_v, weights_v, sems,
):
    @pl.when(is_ocean())
    def _():
        rows, size = surface_v.shape
        even = is_even("gx")
        near = jnp.where(even, rows - NEAR, 0)
        copies = fetch(
            sems,
            (surface, surface_v),
            (diffusion, diffusion_v),
            (sea, sea_v),
            (profile.at[0, 0], level_v),
            (sources, sources_v),
            (weights.at[pl.ds(near, NEAR)], weights_v.at[0]),
            (weights.at[pl.ds(rows - NEAR - near, NEAR)], weights_v.at[1]),
        )
        for copy in copies:
            copy.wait()
        first = jnp.where(even, rows - HALO, 0)
        lowest = level_v[...].astype(f32)
        for n, (out, start) in enumerate(((to_a, first), (to_b, rows - HALO - first))):
            part = pl.ds(pl.multiple_of(start, HALO), HALO)
            out[0:HALO] = surface_v[part]
            out[HALO : 2 * HALO] = diffusion_v[part]
            out[2 * HALO : 3 * HALO] = sea_v[part].astype(f32)
            out[3 * HALO : 4 * HALO] = jnp.where(start == 0, lowest[0:HALO], lowest[rows - HALO : rows])
            out[4 * HALO : 5 * HALO] = jnp.zeros((HALO, size), f32)
            out[4 * HALO : 4 * HALO + 2, 0:rows] = sources_v[...].astype(f32)
            for a in range(NEAR):
                for k in range(2):
                    base = PLANES * HALO + (2 * a + k) * size
                    out[base : base + size] = weights_v[n, a, k].astype(f32)


def import_row(pick_ref, a, first, second):
    row = pick_ref[a : a + 1, :].astype(bf16)
    block = jnp.concatenate([first, second], axis=1)
    return lax.dot_general(row, block, (((1,), (1,)), ((), ())), preferred_element_type=f32)


def chosen_rows(pick, received, index):
    tile = received.shape[1]
    place = iota((index.shape[0], received.shape[0]), 1)
    for k in range(index.shape[1]):
        hot = one_hot(index[:, k : k + 1] == place)
        pick[:, k * tile : (k + 1) * tile] = jnp.dot(hot, received[...], preferred_element_type=f32)


def substep(x, flag, mix):
    deep = x * flag
    both = jnp.concatenate([x - deep, deep], axis=0)
    mixed = jnp.dot(mix, both, preferred_element_type=f32)
    return (0.5 * x.astype(f32) + jnp.tanh(mixed)).astype(bf16)


def with_bottom(x, bottom):
    top = x[0:16].astype(f32)
    top = jnp.where(iota(top.shape, 0) == 0, bottom, top).astype(bf16)
    return jnp.concatenate([top, x[16:]], axis=0)


def flat_rows(grid, first, count):
    return jnp.concatenate([grid[first + r : first + r + 1] for r in range(count)], axis=1)


def first_kernel(
    received, sources, weights, sea, x_ref, flag_ref, mixing, lists_ref, profile,
    message, carry, pick, low_f, level_v, carry_v, sems,
):
    tile = received.shape[1]
    (level,) = fetch(sems, (profile.at[0, 0], level_v))
    chosen_rows(pick, received, upright(sources[...]))
    for a in range(carry_v.shape[0]):
        carry_v[a : a + 1, :] = import_row(pick, a, weights[a, 0], weights[a, 1])
    level.wait()
    lowest = level_v[...].astype(f32)
    flux = sea[...].astype(f32) * (carry_v[...] - lowest)
    kept = pltpu.make_async_copy(carry_v, carry, sems.at[1])

    @pl.when(is_ocean())
    def _():
        carry_v[...] = flux * (1.0 / PASSES)
        kept.start()
        message[...] = jnp.zeros(message.shape, bf16)

    @pl.when(jnp.logical_not(is_ocean()))
    def _():
        kept.start()
        mix = jnp.concatenate([mixing[0], mixing[1]], axis=1)
        bottom = (lowest + flux).astype(bf16).astype(f32)
        per = WIDTH // tile
        for c in range(x_ref.shape[1] // WIDTH):
            cols = slice(c * WIDTH, (c + 1) * WIDTH)
            flag = flag_ref[:, cols]
            x = with_bottom(x_ref[:, cols], flat_rows(bottom, c * per, per))
            for _ in range(PHYS - 1):
                x = substep(x, flag, mix)
            deep = x * flag
            both = jnp.concatenate([x - deep, deep], axis=0)
            mixed = jnp.dot(mix[0:16], both, preferred_element_type=f32)
            last = 0.5 * x[0:16].astype(f32) + jnp.tanh(mixed)
            for r in range(per):
                low_f[c * per + r : c * per + r + 1, :] = last[0:1, r * tile : (r + 1) * tile]
        row = iota((message.shape[0], 1), 0)
        target = (row * 10923) >> 16
        m = row - MESSAGE * target
        wanted = spread(lists_ref[...], target - 1 + (m >> 1), m & 1)
        hot = one_hot(iota((message.shape[0], low_f.shape[0]), 1) == wanted)
        tiles = low_f[...].astype(bf16)
        message[...] = jnp.dot(hot, tiles, preferred_element_type=f32).astype(bf16)

    kept.wait()


def second_kernel(
    carry, x_ref, sea, flag_ref, mixing,
    out, to_a, to_b,
    carry_v, x_v, sea_v, flag_v, mixing_v, sems,
):
    rows = carry_v.shape[0]

    @pl.when(is_ocean())
    def _():
        copies = fetch(sems, (carry, carry_v), (x_ref, out))
        copies[0].wait()
        even = is_even("gx")
        top, bottom = carry_v[0:HALO], carry_v[rows - HALO : rows]
        to_a[...] = jnp.where(even, bottom, top)
        to_b[...] = jnp.where(even, top, bottom)
        copies[1].wait()

    @pl.when(jnp.logical_not(is_ocean()))
    def _():
        pairs = ((carry, carry_v), (sea, sea_v), (mixing, mixing_v), (flag_ref, flag_v), (x_ref, x_v))
        for copy in fetch(sems, *pairs):
            copy.wait()
        mix = jnp.concatenate([mixing_v[0], mixing_v[1]], axis=1)
        sea_f = sea_v[...].astype(f32)
        imported = carry_v[...]
        per = WIDTH // carry_v.shape[1]
        for c in range(x_v.shape[1] // WIDTH):
            cols = slice(c * WIDTH, (c + 1) * WIDTH)
            flag = flag_v[:, cols]
            x = x_v[:, cols]
            wet = flat_rows(sea_f, c * per, per)
            brought = flat_rows(imported, c * per, per)
            for _ in range(2):
                low = x[0:16].astype(f32)[0:1]
                x = with_bottom(x, (low + wet * (brought - low)).astype(bf16).astype(f32))
                for _ in range(PHYS):
                    x = substep(x, flag, mix)
            out[:, cols] = x


def third_kernel(
    received, sources, weights, sea, surface, diffusion, forcing_a, forcing_b,
    profile, forcing, still_a, still_b,
    wide, to_a, to_b,
    pick, imported, level_v, forcing_v, above_v, below_v, sems,
):
    @pl.when(is_ocean())
    def _():
        rows, tile = surface.shape
        even = is_even("gx")
        odd = jnp.logical_not(even)

        @pl.when(even)
        def _():
            fetch(sems, (still_a, below_v), (still_b, above_v))

        @pl.when(odd)
        def _():
            fetch(sems, (still_b, below_v), (still_a, above_v))

        level = pltpu.make_async_copy(profile.at[0, 0], level_v, sems.at[2])
        held = pltpu.make_async_copy(forcing, forcing_v, sems.at[3])
        level.start()
        held.start()

        def places(rows_of, first, count, offset):
            q = upright(rows_of, first, count)
            return (q >> 1) * MESSAGE + (q & 1) + offset

        chosen_rows(pick.at[0:rows], received, places(sources[...], 0, rows, 2))
        for a in range(rows):
            imported[a : a + 1, :] = import_row(pick, a, weights[a, 0], weights[a, 1])
        for n, buffer in enumerate((below_v, above_v)):
            pltpu.make_async_copy(still_a, buffer, sems.at[n]).wait()
        level.wait()
        held.wait()
        part = slice(4 * HALO, 4 * HALO + 2)
        below = places(below_v[part, 0:rows].astype(jnp.int32), 0, HALO, 4)
        above = places(above_v[part, 0:rows].astype(jnp.int32), rows - HALO, HALO, 0)
        total = rows + 2 * HALO
        chosen_rows(pick.at[rows:total], received, jnp.concatenate([below, above], axis=0))
        imported[rows:total] = jnp.zeros((2 * HALO, tile), f32)
        for still, first in ((below_v, rows), (above_v, total - NEAR)):
            for n in range(NEAR):
                base = PLANES * HALO + 2 * n * tile
                blocks = [still[base + k * tile : base + (k + 1) * tile, :].astype(bf16) for k in range(2)]
                a = first + n
                imported[a : a + 1, :] = import_row(pick, a, blocks[0], blocks[1])

        def plane(own, p):
            part = slice(p * HALO, (p + 1) * HALO)
            return jnp.concatenate([own, below_v[part], above_v[part]], axis=0)

        sea_all = plane(sea[...].astype(f32), 2)
        lowest = plane(level_v[...].astype(f32), 3)
        beyond = (jnp.where(even, forcing_a[...], forcing_b[...]), jnp.where(even, forcing_b[...], forcing_a[...]))
        planes = [
            jnp.concatenate([forcing_v[...], *beyond], axis=0),
            sea_all * (imported[...] - lowest) * (1.0 / PASSES),
            plane(surface[...], 0),
            plane(diffusion[...], 1),
            sea_all,
        ]
        group = iota((total, tile), 1) >> 3
        right = left = planes[0]
        for p, values in enumerate(planes):
            wide[p] = values
            if p:
                right = jnp.where(group == tile // HALO - 1 - p, pltpu.roll(values, tile - HALO * p, 1), right)
                left = jnp.where(group == p, pltpu.roll(values, HALO * p, 1), left)
        even = is_even("gy")
        to_a[...] = jnp.where(even, right, left)
        to_b[...] = jnp.where(even, left, right)


def fourth_kernel(wide, from_a, from_b, surface, out, sems):
    @pl.when(jnp.logical_not(is_ocean()))
    def _():
        fetch(sems, (surface, out))[0].wait()

    @pl.when(is_ocean())
    def _():
        rows, tile = out.shape
        total = wide.shape[1]
        group = iota((total, tile), 1) >> 3
        even = is_even("gy")
        from_right = jnp.where(even, from_a[...], from_b[...])
        from_left = jnp.where(even, from_b[...], from_a[...])
        fields = []
        for p in range(PLANES):
            right, left = from_right, from_left
            if p:
                right = pltpu.roll(right, tile - HALO * p, 1)
                left = pltpu.roll(left, HALO * p, 1)
            beside = jnp.where(group == 0, right, jnp.where(group == tile // HALO - 1, left, 0.0))
            fields.append(jnp.concatenate([wide[p], beside], axis=1))
        forcing_1, forcing_2, height, coefficient, sea = fields
        for forcing in (forcing_1, forcing_2):
            for sweep in range(PASSES):
                around = pltpu.roll(height, total - 1, 0) + pltpu.roll(height, 1, 0)
                around = around + pltpu.roll(height, 2 * tile - 1, 1) + pltpu.roll(height, 1, 1)
                height = sea * (height + coefficient * (around - 4.0 * height) + forcing)
        out[...] = height[0:rows, 0:tile]


def body(
    profile, surface, diffusion, sea_mask, convective, mixing, remap_weights, sources, send_lists
):
    levels, rows, tile = profile.shape[1:]
    cells = rows * tile
    surface_2d = surface.reshape(rows, tile)
    coefficient = diffusion.reshape(rows, tile)
    sea = sea_mask.reshape(rows, tile)
    matrices = mixing.reshape(2, levels, levels)
    weights = remap_weights.reshape(remap_weights.shape[3:])
    wanted = sources.reshape(sources.shape[3:]).T
    lists = send_lists.reshape(send_lists.shape[3:]).T
    slots, senders = lists.shape
    secs = lax.axis_size("sec")
    gx = lax.axis_size("gx")
    gy = lax.axis_size("gy")
    total = rows + 2 * HALO
    grid = (rows, tile)

    def along(axis, count, to_a, to_b):
        base = (secs - 1) * count
        swaps = []
        for start in (0, 1):
            pairs = [(base + i, base + i + 1) for i in range(start, count - 1, 2)]
            swaps.append(pairs + [(t, s) for s, t in pairs])
        return lax.ppermute(to_a, ("sec", axis), swaps[0]), lax.ppermute(to_b, ("sec", axis), swaps[1])

    def semaphores(count):
        return pltpu.SemaphoreType.DMA((count,))

    (chosen,) = call(
        select_kernel,
        "select_tiles",
        [(profile, HBM), (lists, HBM)],
        [((senders * slots, tile), bf16)],
        [VMEM(grid, bf16), VMEM(lists.shape, jnp.int32), semaphores(2)],
    )
    received = lax.all_to_all(chosen.reshape(senders, slots, tile), ("sec", "gx"), 0, 0, tiled=True)

    height = PLANES * HALO + NEAR * 2 * tile
    still_a, still_b = call(
        edges_kernel,
        "edge_rows",
        [(surface_2d, HBM), (coefficient, HBM), (sea, HBM), (profile, HBM), (wanted, HBM), (weights, HBM)],
        [((height, tile), f32)] * 2,
        [
            VMEM(grid, f32),
            VMEM(grid, f32),
            VMEM(grid, jnp.int32),
            VMEM(grid, bf16),
            VMEM(wanted.shape, jnp.int32),
            VMEM((2, NEAR, 2, tile, tile), bf16),
            semaphores(7),
        ],
    )
    still_a, still_b = along("gx", gx, still_a, still_b)

    columns = profile.reshape(levels, cells)
    flag = convective.reshape(1, cells).astype(bf16)
    message, carry = call(
        first_kernel,
        "first_step",
        [
            received.reshape(senders * slots, tile), wanted, weights, sea, (columns, VMEM), flag,
            matrices, lists, (profile, HBM),
        ],
        [((senders * MESSAGE, tile), bf16), (grid, f32, HBM)],
        [VMEM((rows, 2 * tile), f32), VMEM(grid, f32), VMEM(grid, bf16), VMEM(grid, f32), semaphores(2)],
        flops=1 << 34,
    )
    again = lax.all_to_all(
        message.reshape(senders * MESSAGE // 2, 2, tile), ("sec", "gx"), 0, 0, tiled=True
    )
    final, forcing_a, forcing_b = call(
        second_kernel,
        "second_step",
        [(carry, HBM), (columns, HBM), (sea, HBM), (flag, HBM), (matrices, HBM)],
        [((levels, cells), bf16), ((HALO, tile), f32), ((HALO, tile), f32)],
        [
            VMEM(grid, f32),
            VMEM((levels, cells), bf16),
            VMEM(grid, jnp.int32),
            VMEM((1, cells), bf16),
            VMEM(matrices.shape, bf16),
            semaphores(5),
        ],
        flops=1 << 34,
    )
    forcing_a, forcing_b = along("gx", gx, forcing_a, forcing_b)

    wide, to_a, to_b = call(
        third_kernel,
        "second_import",
        [
            again.reshape(senders * MESSAGE, tile), wanted, weights, sea, surface_2d, coefficient,
            forcing_a, forcing_b, (profile, HBM), (carry, HBM), (still_a, HBM), (still_b, HBM),
        ],
        [((PLANES, total, tile), f32), ((total, tile), f32), ((total, tile), f32)],
        [
            VMEM((total, 2 * tile), f32),
            VMEM((total, tile), f32),
            VMEM(grid, bf16),
            VMEM(grid, f32),
            VMEM((height, tile), f32),
            VMEM((height, tile), f32),
            semaphores(4),
        ],
    )
    from_a, from_b = along("gy", gy, to_a, to_b)
    (surface_out,) = call(
        fourth_kernel,
        "passes",
        [wide, from_a, from_b, (surface_2d, HBM)],
        [(grid, f32)],
        [semaphores(1)],
    )
    return (final.reshape(profile.shape), surface_out.reshape(surface.shape))


def solution(mesh):
    return jax.shard_map(
        body,
        mesh=mesh,
        in_specs=(
            P("sec", None, "gx", "gy"),
            P("sec", "gx", "gy"),
            P("sec", "gx", "gy"),
            P("sec", "gx", "gy"),
            P("sec", "gx", "gy"),
            P("sec", None, None, None),
            P("sec", "gx", "gy", None, None, None, None),
            P("sec", "gx", "gy", None, None),
            P("sec", "gx", "gy", None, None),
        ),
        out_specs=(P("sec", None, "gx", "gy"), P("sec", "gx", "gy")),
        check_vma=False,
    )
```

```python
import functools

import jax
import jax.numpy as jnp
from jax import lax
from jax.experimental import pallas as pl
from jax.experimental.pallas import tpu as pltpu
from jax.sharding import PartitionSpec as P

PHYS = 4
PASSES = 4
HALO = 8
NEAR = 3
PLANES = 5
WIDTH = 2048
MESSAGE = 8
bf16 = jnp.bfloat16
f32 = jnp.float32
HBM = pltpu.HBM
VMEM = pltpu.VMEM
VMEM_LIMIT = 16 * 1024 * 1024


def call(kernel, name, operands, outs, scratch=(), flops=0, aliases=None):
    values, specs = [], []
    for operand in operands:
        value, place = operand if isinstance(operand, tuple) else (operand, None)
        if place is not None:
            value = pltpu.with_memory_space_constraint(value, place)
        values.append(value)
        specs.append(pl.BlockSpec(memory_space=HBM if place is HBM else VMEM))
    shapes = [
        out[2](out[0], out[1]) if len(out) > 2 else jax.ShapeDtypeStruct(out[0], out[1]) for out in outs
    ]
    return pl.pallas_call(
        kernel,
        out_shape=shapes,
        in_specs=specs,
        out_specs=[pl.BlockSpec(memory_space=out[2] if len(out) > 2 else VMEM) for out in outs],
        scratch_shapes=list(scratch),
        input_output_aliases=aliases or {},
        name=name,
        cost_estimate=pl.CostEstimate(flops=flops, bytes_accessed=1 << 20, transcendentals=0),
        compiler_params=pltpu.CompilerParams(vmem_limit_bytes=VMEM_LIMIT),
    )(*values)


def fetch(sems, *pairs):
    copies = [pltpu.make_async_copy(source, target, sems.at[n]) for n, (source, target) in enumerate(pairs)]
    for copy in copies:
        copy.start()
    return copies


def is_ocean():
    return lax.axis_index("sec") == lax.axis_size("sec") - 1


def is_even(axis):
    return lax.rem(lax.axis_index(axis), 2) == 0


def iota(shape, dim):
    return lax.broadcasted_iota(jnp.int32, shape, dim)


def one_hot(flags):
    return jnp.where(flags, 1.0, 0.0).astype(bf16)


def spread(rows, column, odd):
    hot = one_hot(iota((column.shape[0], rows.shape[1]), 1) == column)
    values = rows.astype(f32).astype(bf16)
    both = lax.dot_general(hot, values, (((1,), (1,)), ((), ())), preferred_element_type=f32)
    return jnp.where(odd == 1, both[:, 1:2], both[:, 0:1]).astype(jnp.int32)


def upright(rows, first=0, count=None):
    count = rows.shape[1] if count is None else count
    unit = one_hot(iota((count, rows.shape[1]), 0) + first == iota((count, rows.shape[1]), 1))
    values = rows.astype(f32).astype(bf16)
    turned = lax.dot_general(unit, values, (((1,), (1,)), ((), ())), preferred_element_type=f32)
    return turned.astype(jnp.int32)


def select_kernel(profile, lists_ref, out_ref, lowest, tiles_v, lists_v, sems):
    copies = fetch(sems, (lists_ref, lists_v), (profile.at[0, 0], tiles_v))
    row = iota((out_ref.shape[0], 1), 0)
    copies[0].wait()
    tile = spread(lists_v[...], row >> 1, row & 1)
    hot = one_hot(iota((out_ref.shape[0], tiles_v.shape[0]), 1) == tile)
    copies[1].wait()
    tiles = tiles_v[...]
    out_ref[...] = jnp.dot(hot, tiles, preferred_element_type=f32).astype(bf16)
    lowest[...] = tiles.astype(f32)


def parts(values):
    high = values.astype(bf16).astype(f32)
    rest = values - high
    middle = rest.astype(bf16).astype(f32)
    return [high, middle, rest - middle]


def edges_kernel(
    surface, diffusion, sea, profile, sources, weights, lists, to_a, to_b, hot, hot_message,
    surface_v, diffusion_v, sea_v, level_v, sources_v, lists_v, edge_v, hot_v, sems,
):
    rows, size = surface_v.shape
    count = 2 * NEAR
    last = is_even("gx")
    near = jnp.where(last, 2 * rows - count, 0)
    pairs = (
        (weights.at[pl.ds(near, count)], edge_v.at[0, 0:count]),
        (weights.at[pl.ds(2 * rows - count - near, count)], edge_v.at[1, 0:count]),
        (surface, surface_v),
        (diffusion, diffusion_v),
        (sea, sea_v),
        (profile.at[0, 0], level_v),
        (sources, sources_v),
        (lists, lists_v),
    )
    copies = [pltpu.make_async_copy(source, target, sems.at[n]) for n, (source, target) in enumerate(pairs)]
    copies[-2].start()
    copies[-1].start()

    @pl.when(is_ocean())
    def _():
        for copy in copies[:-2]:
            copy.start()

    row = iota((hot_v.shape[0], 1), 0)
    target, m = row >> 3, row & 7
    own = lax.axis_index("sec") * lax.axis_size("gx") + lax.axis_index("gx")
    of_edge = jnp.where(target == own + 1, rows - HALO + m, jnp.where(target == own - 1, m, -1))
    copies[-2].wait()
    copies[-1].wait()
    of_tiles = spread(lists_v[...], target - 1 + (m >> 1), m & 1)
    wanted = jnp.where(is_ocean(), of_edge, of_tiles)
    hot_v[...] = one_hot(iota(hot_v.shape, 1) == wanted)
    sent = pltpu.make_async_copy(hot_v, hot_message, sems.at[len(copies)])
    sent.start()
    q = upright(sources_v[...])
    place = iota((rows, hot.shape[1]), 1)
    hot[...] = jnp.concatenate([one_hot(q[:, k : k + 1] == place) for k in (0, 1)], axis=0)

    @pl.when(is_ocean())
    def _():
        for copy in copies[2:-2]:
            copy.wait()
        held = jnp.concatenate([sources_v[...].astype(f32), jnp.zeros((2, size - rows), f32)], axis=1)
        fields = (
            *parts(surface_v[...]),
            *parts(diffusion_v[...]),
            sea_v[...].astype(f32),
            level_v[...].astype(f32),
        )
        for n in (0, 1):
            tail = last if n == 0 else jnp.logical_not(last)
            pieces = [jnp.where(tail, v[rows - HALO : rows], v[0:HALO]) for v in fields] + [held]
            used = sum(piece.shape[0] for piece in pieces)
            pieces.append(jnp.zeros((size - used, size), f32))
            edge_v[n, count] = jnp.concatenate(pieces, axis=0).astype(bf16)
        copies[0].wait()
        copies[1].wait()
        for copy in fetch(sems, (edge_v.at[0], to_a), (edge_v.at[1], to_b)):
            copy.wait()

    sent.wait()


def pass_kernel(edge, *refs):
    pass


def import_row(pick_ref, a, first, second):
    row = pick_ref[a : a + 1, :].astype(bf16)
    block = jnp.concatenate([first, second], axis=1)
    return lax.dot_general(row, block, (((1,), (1,)), ((), ())), preferred_element_type=f32)


def substep(x, flag, mix):
    deep = x * flag
    both = jnp.concatenate([x - deep, deep], axis=0)
    mixed = jnp.dot(mix, both, preferred_element_type=f32)
    return (0.5 * x.astype(f32) + jnp.tanh(mixed)).astype(bf16)


def with_bottom(x, bottom):
    top = x[0:16].astype(f32)
    top = jnp.where(iota(top.shape, 0) == 0, bottom, top).astype(bf16)
    return jnp.concatenate([top, x[16:]], axis=0)


def flat_rows(grid, first, count):
    return jnp.concatenate([grid[first + r : first + r + 1] for r in range(count)], axis=1)


def first_kernel(
    received, hot, weights, lowest_ref, sea, x_ref, flag_ref, mixing, hot_message,
    message, carry, pick, low_f, carry_v, hot_v, sems,
):
    rows, tile = carry_v.shape
    pltpu.make_async_copy(hot_message, hot_v, sems.at[1]).start()
    picked = jnp.dot(hot[...], received[...], preferred_element_type=f32)
    pick[:, 0:tile] = picked[0:rows]
    pick[:, tile : 2 * tile] = picked[rows : 2 * rows]
    for a in range(rows):
        carry_v[a : a + 1, :] = import_row(pick, a, weights[2 * a], weights[2 * a + 1])
    lowest = lowest_ref[...]
    flux = sea[...].astype(f32) * (carry_v[...] - lowest)
    kept = pltpu.make_async_copy(carry_v, carry, sems.at[0])

    def send(rows_of):
        pltpu.make_async_copy(hot_message, hot_v, sems.at[1]).wait()
        made = jnp.dot(hot_v[...], rows_of.astype(bf16), preferred_element_type=f32)
        message[...] = made.astype(bf16)

    @pl.when(is_ocean())
    def _():
        forcing = flux * (1.0 / PASSES)
        carry_v[...] = forcing
        kept.start()
        send(forcing)

    @pl.when(jnp.logical_not(is_ocean()))
    def _():
        kept.start()
        mix = jnp.concatenate([mixing[0], mixing[1]], axis=1)
        bottom = (lowest + flux).astype(bf16).astype(f32)
        per = WIDTH // tile
        for c in range(x_ref.shape[1] // WIDTH):
            cols = slice(c * WIDTH, (c + 1) * WIDTH)
            flag = flag_ref[:, cols]
            x = with_bottom(x_ref[:, cols], flat_rows(bottom, c * per, per))
            for _ in range(PHYS - 1):
                x = substep(x, flag, mix)
            deep = x * flag
            both = jnp.concatenate([x - deep, deep], axis=0)
            mixed = jnp.dot(mix[0:16], both, preferred_element_type=f32)
            last = 0.5 * x[0:16].astype(f32) + jnp.tanh(mixed)
            for r in range(per):
                low_f[c * per + r : c * per + r + 1, :] = last[0:1, r * tile : (r + 1) * tile]
        send(low_f[...])

    kept.wait()


def second_kernel(
    carry, x_ref, flag_ref, mixing, sea, out, made, carry_v, x_v, flag_v, mixing_v, sea_v, sems
):
    made[...] = jnp.zeros(made.shape, f32)

    @pl.when(is_ocean())
    def _():
        fetch(sems, (x_ref, x_v))[0].wait()
        fetch(sems, (x_v, out))[0].wait()

    @pl.when(jnp.logical_not(is_ocean()))
    def _():
        pairs = ((carry, carry_v), (sea, sea_v), (mixing, mixing_v), (flag_ref, flag_v), (x_ref, x_v))
        for copy in fetch(sems, *pairs):
            copy.wait()
        mix = jnp.concatenate([mixing_v[0], mixing_v[1]], axis=1)
        sea_f = sea_v[...].astype(f32)
        imported = carry_v[...]
        per = WIDTH // carry_v.shape[1]
        for c in range(x_v.shape[1] // WIDTH):
            cols = slice(c * WIDTH, (c + 1) * WIDTH)
            flag = flag_v[:, cols]
            x = x_v[:, cols]
            wet = flat_rows(sea_f, c * per, per)
            brought = flat_rows(imported, c * per, per)
            for _ in range(2):
                low = x[0:16].astype(f32)[0:1]
                x = with_bottom(x, (low + wet * (brought - low)).astype(bf16).astype(f32))
                for _ in range(PHYS):
                    x = substep(x, flag, mix)
            x_v[:, cols] = x
        fetch(sems, (x_v, out))[0].wait()


def ready_kernel(
    surface, diffusion, sea, profile, sources, carry, still_a, still_b, made,
    hot, planes,
    surface_v, diffusion_v, sea_v, level_v, sources_v, carry_v, sems,
):
    @pl.when(is_ocean())
    def _():
        rows, tile = surface_v.shape
        total = rows + 2 * HALO
        even = is_even("gx")

        copies = fetch(
            sems,
            (surface, surface_v),
            (diffusion, diffusion_v),
            (sea, sea_v),
            (profile.at[0, 0], level_v),
            (sources, sources_v),
            (carry, carry_v),
        )
        for copy in copies:
            copy.wait()
        edges = [still[2 * NEAR].astype(f32) for still in (still_a, still_b)]
        below = jnp.where(even, edges[0], edges[1])
        above = jnp.where(even, edges[1], edges[0])

        def whole_of(values, at, pieces):
            held = [below[at : at + HALO], above[at : at + HALO]]
            for n in range(1, pieces):
                part = slice(at + n * HALO, at + (n + 1) * HALO)
                held = [held[0] + below[part], held[1] + above[part]]
            return jnp.concatenate([values, *held], axis=0)

        planes[0] = whole_of(surface_v[...], 0, 3)
        planes[1] = whole_of(diffusion_v[...], 3 * HALO, 3)
        planes[2] = whole_of(sea_v[...].astype(f32), 6 * HALO, 1)
        planes[3] = whole_of(level_v[...].astype(f32), 7 * HALO, 1)
        planes[4, 0:rows] = carry_v[...]
        planes[4, rows:total] = jnp.zeros((2 * HALO, tile), f32)

        at = slice(8 * HALO, 8 * HALO + 2)
        q = jnp.concatenate(
            [
                upright(sources_v[...]),
                upright(below[at, 0:rows].astype(jnp.int32), 0, HALO),
                upright(above[at, 0:rows].astype(jnp.int32), rows - HALO, HALO),
            ],
            axis=0,
        )
        row = iota((total, 1), 0)
        offset = jnp.where(row < rows, 2, jnp.where(row < rows + HALO, 4, 0))
        place = iota((total, hot.shape[1]), 1)
        q = (q >> 1) * MESSAGE + (q & 1) + offset
        own = lax.axis_index("sec") * lax.axis_size("gx") + lax.axis_index("gx")
        row = iota((2 * HALO, 1), 0)
        beyond = jnp.where(row < HALO, (own + 1) * MESSAGE, (own - 1) * MESSAGE - HALO) + row
        place_b = iota((2 * HALO, hot.shape[1]), 1)
        hot[...] = jnp.concatenate(
            [one_hot(q[:, 0:1] == place), one_hot(q[:, 1:2] == place), one_hot(beyond == place_b)], axis=0
        )


def third_kernel(
    received, weights, hot, planes, still_a, still_b, wide, to_a, to_b, pick, imported
):
    @pl.when(is_ocean())
    def _():
        total, tile = imported.shape
        rows = total - 2 * HALO
        picked = jnp.dot(hot[...], received[...], preferred_element_type=f32)
        pick[:, 0:tile] = picked[0:total]
        pick[:, tile : 2 * tile] = picked[total : 2 * total]
        imported[rows:total] = jnp.zeros((2 * HALO, tile), f32)
        for a in range(rows):
            imported[a : a + 1, :] = import_row(pick, a, weights[2 * a], weights[2 * a + 1])
        from_next = is_even("gx")
        for n in range(NEAR):
            for a, first in ((rows + n, from_next), (total - NEAR + n, jnp.logical_not(from_next))):
                blocks = [jnp.where(first, still_a[2 * n + k], still_b[2 * n + k]) for k in range(2)]
                imported[a : a + 1, :] = import_row(pick, a, blocks[0], blocks[1])
        fields = [
            jnp.concatenate([planes[4, 0:rows], picked[2 * total :]], axis=0),
            planes[2] * (imported[...] - planes[3]) * (1.0 / PASSES),
            planes[0],
            planes[1],
            planes[2],
        ]
        group = iota((total, tile), 1) >> 3
        right = left = fields[0]
        for p, values in enumerate(fields):
            wide[p] = values
            if p:
                right = jnp.where(group == tile // HALO - 1 - p, pltpu.roll(values, tile - HALO * p, 1), right)
                left = jnp.where(group == p, pltpu.roll(values, HALO * p, 1), left)
        even = is_even("gy")
        to_a[...] = jnp.where(even, right, left)
        to_b[...] = jnp.where(even, left, right)


def fourth_kernel(wide, from_a, from_b, surface, out, sems):
    @pl.when(jnp.logical_not(is_ocean()))
    def _():
        fetch(sems, (surface, out))[0].wait()

    @pl.when(is_ocean())
    def _():
        rows, tile = out.shape
        total = wide.shape[1]
        group = iota((total, tile), 1) >> 3
        even = is_even("gy")
        from_right = jnp.where(even, from_a[...], from_b[...])
        from_left = jnp.where(even, from_b[...], from_a[...])
        fields = []
        for p in range(PLANES):
            right, left = from_right, from_left
            if p:
                right = pltpu.roll(right, tile - HALO * p, 1)
                left = pltpu.roll(left, HALO * p, 1)
            beside = jnp.where(group == 0, right, jnp.where(group == tile // HALO - 1, left, 0.0))
            fields.append(jnp.concatenate([wide[p], beside], axis=1))
        forcing_1, forcing_2, height, coefficient, sea = fields
        for forcing in (forcing_1, forcing_2):
            for sweep in range(PASSES):
                around = pltpu.roll(height, total - 1, 0) + pltpu.roll(height, 1, 0)
                around = around + pltpu.roll(height, 2 * tile - 1, 1) + pltpu.roll(height, 1, 1)
                height = sea * (height + coefficient * (around - 4.0 * height) + forcing)
        out[...] = height[0:rows, 0:tile]


def body(
    profile, surface, diffusion, sea_mask, convective, mixing, remap_weights, sources, send_lists
):
    levels, rows, tile = profile.shape[1:]
    cells = rows * tile
    surface_2d = surface.reshape(rows, tile)
    coefficient = diffusion.reshape(rows, tile)
    sea = sea_mask.reshape(rows, tile)
    matrices = mixing.reshape(2, levels, levels)
    weights = remap_weights.reshape(2 * rows, tile, tile)
    wanted = sources.reshape(sources.shape[3:]).T
    lists = send_lists.reshape(send_lists.shape[3:]).T
    slots, senders = lists.shape
    secs = lax.axis_size("sec")
    gx = lax.axis_size("gx")
    gy = lax.axis_size("gy")
    total = rows + 2 * HALO
    grid = (rows, tile)

    base = {"gx": (secs - 1) * gx, "gy": (secs - 1) * gy}
    counts = {"gx": gx, "gy": gy}

    def swap(axis, start, values):
        first = base[axis]
        pairs = [(first + i, first + i + 1) for i in range(start, counts[axis] - 1, 2)]
        return lax.ppermute(values, ("sec", axis), pairs + [(t, s) for s, t in pairs])

    def semaphores(count):
        return pltpu.SemaphoreType.DMA((count,))

    chosen, lowest = call(
        select_kernel,
        "select_tiles",
        [(profile, HBM), (lists, HBM)],
        [((senders * slots, tile), bf16), (grid, f32)],
        [VMEM(grid, bf16), VMEM(lists.shape, jnp.int32), semaphores(2)],
    )
    received = lax.all_to_all(chosen.reshape(senders, slots, tile), ("sec", "gx"), 0, 0, tiled=True)

    edge = ((2 * NEAR + 1, tile, tile), bf16, HBM)
    edge_operands = [(v, HBM) for v in (surface_2d, coefficient, sea, profile, wanted, weights)]
    edge_scratch = [
        VMEM(grid, f32),
        VMEM(grid, f32),
        VMEM(grid, jnp.int32),
        VMEM(grid, bf16),
        VMEM(wanted.shape, jnp.int32),
    ]
    edge_a, edge_b, hot_first, hot_message = call(
        edges_kernel,
        "edge_rows",
        [*edge_operands, (lists, HBM)],
        [edge, edge, ((2 * rows, senders * slots), bf16), ((senders * MESSAGE, rows), bf16, HBM)],
        [
            *edge_scratch,
            VMEM(lists.shape, jnp.int32),
            VMEM((2, *edge[0]), bf16),
            VMEM((senders * MESSAGE, rows), bf16),
            semaphores(9),
        ],
    )
    still_a = swap("gx", 0, edge_a)

    columns = profile.reshape(levels, cells)
    flag = convective.reshape(1, cells).astype(bf16)
    message, carry = call(
        first_kernel,
        "first_step",
        [
            received.reshape(senders * slots, tile), hot_first, weights, lowest, sea, (columns, VMEM),
            flag, matrices, (hot_message, HBM),
        ],
        [((senders * MESSAGE, tile), bf16), (grid, f32, HBM)],
        [
            VMEM((rows, 2 * tile), f32),
            VMEM(grid, f32),
            VMEM(grid, f32),
            VMEM((senders * MESSAGE, rows), bf16),
            semaphores(2),
        ],
        flops=1 << 34,
    )
    again = lax.all_to_all(
        message.reshape(senders * MESSAGE // 2, 2, tile), ("sec", "gx"), 0, 0, tiled=True
    )
    (edge_b,) = call(pass_kernel, "pass_edge", [(edge_b, HBM), (carry, HBM), still_a], [edge], aliases={0: 0})
    still_b = swap("gx", 1, edge_b)
    final, made = call(
        second_kernel,
        "second_step",
        [(carry, HBM), (columns, HBM), (flag, HBM), (matrices, HBM), (sea, HBM)],
        [((levels, cells), bf16, HBM), ((8, tile), f32)],
        [
            VMEM(grid, f32),
            VMEM((levels, cells), bf16),
            VMEM((1, cells), bf16),
            VMEM(matrices.shape, bf16),
            VMEM(grid, jnp.int32),
            semaphores(5),
        ],
        flops=1 << 34,
    )
    picks = 2 * total + 2 * HALO
    hot, planes = call(
        ready_kernel,
        "ready_import",
        [*edge_operands[:5], (carry, HBM), still_a, still_b, made],
        [((picks, senders * MESSAGE), bf16), ((PLANES, total, tile), f32)],
        [*edge_scratch, VMEM(grid, f32), semaphores(6)],
    )
    wide, to_a, to_b = call(
        third_kernel,
        "second_import",
        [again.reshape(senders * MESSAGE, tile), weights, hot, planes, still_a, still_b],
        [((PLANES, total, tile), f32), ((total, tile), f32), ((total, tile), f32)],
        [
            VMEM((total, 2 * tile), f32),
            VMEM((total, tile), f32),
        ],
    )
    from_a, from_b = swap("gy", 0, to_a), swap("gy", 1, to_b)
    (surface_out,) = call(
        fourth_kernel,
        "passes",
        [wide, from_a, from_b, (surface_2d, HBM)],
        [(grid, f32)],
        [semaphores(1)],
    )
    return (final.reshape(profile.shape), surface_out.reshape(surface.shape))


def solution(mesh):
    return jax.shard_map(
        body,
        mesh=mesh,
        in_specs=(
            P("sec", None, "gx", "gy"),
            P("sec", "gx", "gy"),
            P("sec", "gx", "gy"),
            P("sec", "gx", "gy"),
            P("sec", "gx", "gy"),
            P("sec", None, None, None),
            P("sec", "gx", "gy", None, None, None, None),
            P("sec", "gx", "gy", None, None),
            P("sec", "gx", "gy", None, None),
        ),
        out_specs=(P("sec", None, "gx", "gy"), P("sec", "gx", "gy")),
        check_vma=False,
    )
```

```python
import functools

import jax
import jax.numpy as jnp
from jax import lax
from jax.experimental import pallas as pl
from jax.experimental.pallas import tpu as pltpu
from jax.sharding import PartitionSpec as P

PHYS = 4
PASSES = 4
HALO = 8
NEAR = 3
PLANES = 5
WIDTH = 2048
PIECES = 8
MESSAGE = 8
bf16 = jnp.bfloat16
f32 = jnp.float32
HBM = pltpu.HBM
VMEM = pltpu.VMEM
VMEM_LIMIT = 16 * 1024 * 1024


def call(kernel, name, operands, outs, scratch=(), flops=0, aliases=None):
    values, specs = [], []
    for operand in operands:
        value, place = operand if isinstance(operand, tuple) else (operand, None)
        if place is not None:
            value = pltpu.with_memory_space_constraint(value, place)
        values.append(value)
        specs.append(pl.BlockSpec(memory_space=HBM if place is HBM else VMEM))
    shapes = [
        out[2](out[0], out[1]) if len(out) > 2 else jax.ShapeDtypeStruct(out[0], out[1]) for out in outs
    ]
    return pl.pallas_call(
        kernel,
        out_shape=shapes,
        in_specs=specs,
        out_specs=[pl.BlockSpec(memory_space=out[2] if len(out) > 2 else VMEM) for out in outs],
        scratch_shapes=list(scratch),
        input_output_aliases=aliases or {},
        name=name,
        cost_estimate=pl.CostEstimate(flops=flops, bytes_accessed=1 << 20, transcendentals=0),
        compiler_params=pltpu.CompilerParams(vmem_limit_bytes=VMEM_LIMIT),
    )(*values)


def fetch(sems, *pairs):
    copies = [pltpu.make_async_copy(source, target, sems.at[n]) for n, (source, target) in enumerate(pairs)]
    for copy in copies:
        copy.start()
    return copies


def pieces(source, target):
    size = source.shape[0] // PIECES
    return [(source.at[n * size : (n + 1) * size], target.at[n * size : (n + 1) * size]) for n in range(PIECES)]


def is_ocean():
    return lax.axis_index("sec") == lax.axis_size("sec") - 1


def is_even(axis):
    return lax.rem(lax.axis_index(axis), 2) == 0


def iota(shape, dim):
    return lax.broadcasted_iota(jnp.int32, shape, dim)


def one_hot(flags):
    return jnp.where(flags, 1.0, 0.0).astype(bf16)


def spread(rows, column, odd):
    hot = one_hot(iota((column.shape[0], rows.shape[1]), 1) == column)
    values = rows.astype(f32).astype(bf16)
    both = lax.dot_general(hot, values, (((1,), (1,)), ((), ())), preferred_element_type=f32)
    return jnp.where(odd == 1, both[:, 1:2], both[:, 0:1]).astype(jnp.int32)


def upright(rows, first=0, count=None):
    count = rows.shape[1] if count is None else count
    unit = one_hot(iota((count, rows.shape[1]), 0) + first == iota((count, rows.shape[1]), 1))
    values = rows.astype(f32).astype(bf16)
    turned = lax.dot_general(unit, values, (((1,), (1,)), ((), ())), preferred_element_type=f32)
    return turned.astype(jnp.int32)


def select_kernel(profile, lists_ref, out_ref, lowest, tiles_v, lists_v, sems):
    copies = fetch(sems, (lists_ref, lists_v), (profile.at[0, 0], tiles_v))
    row = iota((out_ref.shape[0], 1), 0)
    copies[0].wait()
    tile = spread(lists_v[...], row >> 1, row & 1)
    hot = one_hot(iota((out_ref.shape[0], tiles_v.shape[0]), 1) == tile)
    copies[1].wait()
    tiles = tiles_v[...]
    out_ref[...] = jnp.dot(hot, tiles, preferred_element_type=f32).astype(bf16)
    lowest[...] = tiles.astype(f32)


def parts(values):
    high = values.astype(bf16).astype(f32)
    rest = values - high
    middle = rest.astype(bf16).astype(f32)
    return [high, middle, rest - middle]


def edges_kernel(
    surface, diffusion, sea, profile, sources, weights, lists, to_a, to_b, hot, hot_message,
    surface_v, diffusion_v, sea_v, level_v, sources_v, lists_v, edge_v, hot_v, sems,
):
    rows, size = surface_v.shape
    count = 2 * NEAR
    last = is_even("gx")
    near = jnp.where(last, 2 * rows - count, 0)
    pairs = (
        (weights.at[pl.ds(near, count)], edge_v.at[0, 0:count]),
        (weights.at[pl.ds(2 * rows - count - near, count)], edge_v.at[1, 0:count]),
        (surface, surface_v),
        (diffusion, diffusion_v),
        (sea, sea_v),
        (profile.at[0, 0], level_v),
        (sources, sources_v),
        (lists, lists_v),
    )
    copies = [pltpu.make_async_copy(source, target, sems.at[n]) for n, (source, target) in enumerate(pairs)]
    copies[-2].start()
    copies[-1].start()

    @pl.when(is_ocean())
    def _():
        for copy in copies[:-2]:
            copy.start()

    row = iota((hot_v.shape[0], 1), 0)
    target, m = (row >> 3) + lists_v.shape[1] - lax.axis_size("gx"), row & 7
    own = lax.axis_index("sec") * lax.axis_size("gx") + lax.axis_index("gx")
    of_edge = jnp.where(target == own + 1, rows - HALO + m, jnp.where(target == own - 1, m, -1))
    copies[-2].wait()
    copies[-1].wait()
    of_tiles = spread(lists_v[...], target - 1 + (m >> 1), m & 1)
    wanted = jnp.where(is_ocean(), of_edge, of_tiles)
    hot_v[...] = one_hot(iota(hot_v.shape, 1) == wanted)
    sent = pltpu.make_async_copy(hot_v, hot_message, sems.at[len(copies)])
    sent.start()
    q = upright(sources_v[...])
    place = iota((rows, hot.shape[1]), 1)
    hot[...] = jnp.concatenate([one_hot(q[:, k : k + 1] == place) for k in (0, 1)], axis=0)

    @pl.when(is_ocean())
    def _():
        for copy in copies[2:-2]:
            copy.wait()
        held = jnp.concatenate([sources_v[...].astype(f32), jnp.zeros((2, size - rows), f32)], axis=1)
        fields = (
            *parts(surface_v[...]),
            *parts(diffusion_v[...]),
            sea_v[...].astype(f32),
            level_v[...].astype(f32),
        )
        for n in (0, 1):
            tail = last if n == 0 else jnp.logical_not(last)
            pieces = [jnp.where(tail, v[rows - HALO : rows], v[0:HALO]) for v in fields] + [held]
            used = sum(piece.shape[0] for piece in pieces)
            pieces.append(jnp.zeros((size - used, size), f32))
            edge_v[n, count] = jnp.concatenate(pieces, axis=0).astype(bf16)
        copies[0].wait()
        copies[1].wait()
        for copy in fetch(sems, (edge_v.at[0], to_a), (edge_v.at[1], to_b)):
            copy.wait()

    sent.wait()


def pass_kernel(edge, *refs):
    pass


def import_row(pick_ref, a, first, second):
    row = pick_ref[a : a + 1, :].astype(bf16)
    block = jnp.concatenate([first, second], axis=1)
    return lax.dot_general(row, block, (((1,), (1,)), ((), ())), preferred_element_type=f32)


def substep(x, flag, mix):
    deep = x * flag
    both = jnp.concatenate([x - deep, deep], axis=0)
    mixed = jnp.dot(mix, both, preferred_element_type=f32)
    return (0.5 * x.astype(f32) + jnp.tanh(mixed)).astype(bf16)


def with_bottom(x, bottom):
    top = x[0:16].astype(f32)
    top = jnp.where(iota(top.shape, 0) == 0, bottom, top).astype(bf16)
    return jnp.concatenate([top, x[16:]], axis=0)


def flat_rows(grid, first, count):
    return jnp.concatenate([grid[first + r : first + r + 1] for r in range(count)], axis=1)


def first_kernel(
    received, hot, weights, lowest_ref, sea, x_ref, flag_ref, mixing, hot_message,
    message, carry, pick, low_f, carry_v, hot_v, message_v, sems,
):
    rows, tile = carry_v.shape
    pltpu.make_async_copy(hot_message, hot_v, sems.at[1]).start()
    picked = jnp.dot(hot[...], received[...], preferred_element_type=f32)
    pick[:, 0:tile] = picked[0:rows]
    pick[:, tile : 2 * tile] = picked[rows : 2 * rows]
    for a in range(rows):
        carry_v[a : a + 1, :] = import_row(pick, a, weights[2 * a], weights[2 * a + 1])
    lowest = lowest_ref[...]
    flux = sea[...].astype(f32) * (carry_v[...] - lowest)
    kept = pltpu.make_async_copy(carry_v, carry, sems.at[0])

    def send(rows_of):
        pltpu.make_async_copy(hot_message, hot_v, sems.at[1]).wait()
        made = jnp.dot(hot_v[...], rows_of.astype(bf16), preferred_element_type=f32)
        message_v[...] = made.astype(bf16)
        total, count = message.shape[0], message_v.shape[0]
        (copy,) = fetch(sems.at[2:3], (message_v, message.at[total - count : total]))
        copy.wait()

    @pl.when(is_ocean())
    def _():
        forcing = flux * (1.0 / PASSES)
        carry_v[...] = forcing
        kept.start()
        send(forcing)

    @pl.when(jnp.logical_not(is_ocean()))
    def _():
        kept.start()
        mix = jnp.concatenate([mixing[0], mixing[1]], axis=1)
        bottom = (lowest + flux).astype(bf16).astype(f32)
        per = WIDTH // tile
        for c in range(x_ref.shape[1] // WIDTH):
            cols = slice(c * WIDTH, (c + 1) * WIDTH)
            flag = flag_ref[:, cols]
            x = with_bottom(x_ref[:, cols], flat_rows(bottom, c * per, per))
            for _ in range(PHYS - 1):
                x = substep(x, flag, mix)
            deep = x * flag
            both = jnp.concatenate([x - deep, deep], axis=0)
            mixed = jnp.dot(mix[0:16], both, preferred_element_type=f32)
            last = 0.5 * x[0:16].astype(f32) + jnp.tanh(mixed)
            for r in range(per):
                low_f[c * per + r : c * per + r + 1, :] = last[0:1, r * tile : (r + 1) * tile]
        send(low_f[...])

    kept.wait()


def second_kernel(
    carry, x_ref, flag_ref, mixing, sea, surface, diffusion, profile, sources,
    out, mine, index,
    carry_v, x_v, flag_v, mixing_v, sea_v, level_v, sources_v, sems, x_sems,
):
    @pl.when(is_ocean())
    def _():
        held = fetch(x_sems, *pieces(x_ref, x_v))
        copies = fetch(
            sems,
            (surface, mine.at[0]),
            (diffusion, mine.at[1]),
            (carry, mine.at[4]),
            (sea, sea_v),
            (profile.at[0, 0], level_v),
            (sources, sources_v),
        )
        for copy in copies:
            copy.wait()
        mine[2] = sea_v[...].astype(f32)
        mine[3] = level_v[...].astype(f32)
        q = upright(sources_v[...])
        index[...] = (q >> 1) * MESSAGE + (q & 1) + 2
        for copy in held:
            copy.wait()
        for copy in fetch(x_sems, *pieces(x_v, out)):
            copy.wait()

    @pl.when(jnp.logical_not(is_ocean()))
    def _():
        pairs = ((carry, carry_v), (sea, sea_v), (mixing, mixing_v), (flag_ref, flag_v))
        for copy in fetch(sems, *pairs) + fetch(x_sems, *pieces(x_ref, x_v)):
            copy.wait()
        mix = jnp.concatenate([mixing_v[0], mixing_v[1]], axis=1)
        sea_f = sea_v[...].astype(f32)
        imported = carry_v[...]
        per = WIDTH // carry_v.shape[1]
        for c in range(x_v.shape[1] // WIDTH):
            cols = slice(c * WIDTH, (c + 1) * WIDTH)
            flag = flag_v[:, cols]
            x = x_v[:, cols]
            wet = flat_rows(sea_f, c * per, per)
            brought = flat_rows(imported, c * per, per)
            for _ in range(2):
                low = x[0:16].astype(f32)[0:1]
                x = with_bottom(x, (low + wet * (brought - low)).astype(bf16).astype(f32))
                for _ in range(PHYS):
                    x = substep(x, flag, mix)
            x_v[:, cols] = x
        for copy in fetch(x_sems, *pieces(x_v, out)):
            copy.wait()


def ready_kernel(mine, own_index, still_a, still_b, hot, planes):
    @pl.when(is_ocean())
    def _():
        rows, tile = mine.shape[1:]
        total = rows + 2 * HALO
        even = is_even("gx")
        edges = [still[2 * NEAR].astype(f32) for still in (still_a, still_b)]
        below = jnp.where(even, edges[0], edges[1])
        above = jnp.where(even, edges[1], edges[0])

        def whole_of(values, at, pieces):
            held = [below[at : at + HALO], above[at : at + HALO]]
            for n in range(1, pieces):
                part = slice(at + n * HALO, at + (n + 1) * HALO)
                held = [held[0] + below[part], held[1] + above[part]]
            return jnp.concatenate([values, *held], axis=0)

        planes[0] = whole_of(mine[0], 0, 3)
        planes[1] = whole_of(mine[1], 3 * HALO, 3)
        planes[2] = whole_of(mine[2], 6 * HALO, 1)
        planes[3] = whole_of(mine[3], 7 * HALO, 1)
        planes[4, 0:rows] = mine[4]
        planes[4, rows:total] = jnp.zeros((2 * HALO, tile), f32)

        at = slice(8 * HALO, 8 * HALO + 2)
        held = [own_index[...]]
        for edge, first, offset in ((below, 0, 4), (above, rows - HALO, 0)):
            q = upright(edge[at, 0:rows].astype(jnp.int32), first, HALO)
            held.append((q >> 1) * MESSAGE + (q & 1) + offset)
        q = jnp.concatenate(held, axis=0)
        place = iota((total, hot.shape[1]), 1)
        own = lax.axis_index("sec") * lax.axis_size("gx") + lax.axis_index("gx")
        row = iota((2 * HALO, 1), 0)
        beyond = jnp.where(row < HALO, (own + 1) * MESSAGE, (own - 1) * MESSAGE - HALO) + row
        place_b = iota((2 * HALO, hot.shape[1]), 1)
        hot[...] = jnp.concatenate(
            [one_hot(q[:, 0:1] == place), one_hot(q[:, 1:2] == place), one_hot(beyond == place_b)], axis=0
        )


def third_kernel(
    received, weights, hot, planes, still_a, still_b, wide, to_a, to_b, pick, imported
):
    @pl.when(is_ocean())
    def _():
        total, tile = imported.shape
        rows = total - 2 * HALO
        picked = jnp.dot(hot[...], received[...], preferred_element_type=f32)
        pick[:, 0:tile] = picked[0:total]
        pick[:, tile : 2 * tile] = picked[total : 2 * total]
        imported[rows:total] = jnp.zeros((2 * HALO, tile), f32)
        for a in range(rows):
            imported[a : a + 1, :] = import_row(pick, a, weights[2 * a], weights[2 * a + 1])
        from_next = is_even("gx")
        for n in range(NEAR):
            for a, first in ((rows + n, from_next), (total - NEAR + n, jnp.logical_not(from_next))):
                blocks = [jnp.where(first, still_a[2 * n + k], still_b[2 * n + k]) for k in range(2)]
                imported[a : a + 1, :] = import_row(pick, a, blocks[0], blocks[1])
        fields = [
            jnp.concatenate([planes[4, 0:rows], picked[2 * total :]], axis=0),
            planes[2] * (imported[...] - planes[3]) * (1.0 / PASSES),
            planes[0],
            planes[1],
            planes[2],
        ]
        group = iota((total, tile), 1) >> 3
        right = left = fields[0]
        for p, values in enumerate(fields):
            wide[p] = values
            if p:
                right = jnp.where(group == tile // HALO - 1 - p, pltpu.roll(values, tile - HALO * p, 1), right)
                left = jnp.where(group == p, pltpu.roll(values, HALO * p, 1), left)
        even = is_even("gy")
        to_a[...] = jnp.where(even, right, left)
        to_b[...] = jnp.where(even, left, right)


def fourth_kernel(wide, from_a, from_b, surface, out, sems):
    @pl.when(jnp.logical_not(is_ocean()))
    def _():
        fetch(sems, (surface, out))[0].wait()

    @pl.when(is_ocean())
    def _():
        rows, tile = out.shape
        total = wide.shape[1]
        group = iota((total, tile), 1) >> 3
        even = is_even("gy")
        from_right = jnp.where(even, from_a[...], from_b[...])
        from_left = jnp.where(even, from_b[...], from_a[...])
        fields = []
        for p in range(PLANES):
            right, left = from_right, from_left
            if p:
                right = pltpu.roll(right, tile - HALO * p, 1)
                left = pltpu.roll(left, HALO * p, 1)
            beside = jnp.where(group == 0, right, jnp.where(group == tile // HALO - 1, left, 0.0))
            fields.append(jnp.concatenate([wide[p], beside], axis=1))
        forcing_1, forcing_2, height, coefficient, sea = fields
        for forcing in (forcing_1, forcing_2):
            for sweep in range(PASSES):
                around = pltpu.roll(height, total - 1, 0) + pltpu.roll(height, 1, 0)
                around = around + pltpu.roll(height, 2 * tile - 1, 1) + pltpu.roll(height, 1, 1)
                height = sea * (height + coefficient * (around - 4.0 * height) + forcing)
        out[...] = height[0:rows, 0:tile]


def body(
    profile, surface, diffusion, sea_mask, convective, mixing, remap_weights, sources, send_lists
):
    levels, rows, tile = profile.shape[1:]
    cells = rows * tile
    surface_2d = surface.reshape(rows, tile)
    coefficient = diffusion.reshape(rows, tile)
    sea = sea_mask.reshape(rows, tile)
    matrices = mixing.reshape(2, levels, levels)
    weights = remap_weights.reshape(2 * rows, tile, tile)
    wanted = sources.reshape(sources.shape[3:]).T
    lists = send_lists.reshape(send_lists.shape[3:]).T
    slots, senders = lists.shape
    secs = lax.axis_size("sec")
    gx = lax.axis_size("gx")
    gy = lax.axis_size("gy")
    total = rows + 2 * HALO
    grid = (rows, tile)

    base = {"gx": (secs - 1) * gx, "gy": (secs - 1) * gy}
    counts = {"gx": gx, "gy": gy}

    def swap(axis, start, values):
        first = base[axis]
        pairs = [(first + i, first + i + 1) for i in range(start, counts[axis] - 1, 2)]
        return lax.ppermute(values, ("sec", axis), pairs + [(t, s) for s, t in pairs])

    def semaphores(count):
        return pltpu.SemaphoreType.DMA((count,))

    chosen, lowest = call(
        select_kernel,
        "select_tiles",
        [(profile, HBM), (lists, HBM)],
        [((senders * slots, tile), bf16), (grid, f32)],
        [VMEM(grid, bf16), VMEM(lists.shape, jnp.int32), semaphores(2)],
    )
    received = lax.all_to_all(chosen.reshape(senders, slots, tile), ("sec", "gx"), 0, 0, tiled=True)

    edge = ((2 * NEAR + 1, tile, tile), bf16, HBM)
    edge_operands = [(v, HBM) for v in (surface_2d, coefficient, sea, profile, wanted, weights)]
    edge_scratch = [
        VMEM(grid, f32),
        VMEM(grid, f32),
        VMEM(grid, jnp.int32),
        VMEM(grid, bf16),
        VMEM(wanted.shape, jnp.int32),
    ]
    edge_a, edge_b, hot_first, hot_message = call(
        edges_kernel,
        "edge_rows",
        [*edge_operands, (lists, HBM)],
        [edge, edge, ((2 * rows, senders * slots), bf16), ((gx * MESSAGE, rows), bf16, HBM)],
        [
            *edge_scratch,
            VMEM(lists.shape, jnp.int32),
            VMEM((2, *edge[0]), bf16),
            VMEM((gx * MESSAGE, rows), bf16),
            semaphores(9),
        ],
    )
    still_a = swap("gx", 0, edge_a)

    columns = profile.reshape(levels, cells)
    flag = convective.reshape(1, cells).astype(bf16)
    message, carry = call(
        first_kernel,
        "first_step",
        [
            received.reshape(senders * slots, tile), hot_first, weights, lowest, sea, (columns, VMEM),
            flag, matrices, (hot_message, HBM),
        ],
        [((senders * MESSAGE, tile), bf16, HBM), (grid, f32, HBM)],
        [
            VMEM((rows, 2 * tile), f32),
            VMEM(grid, f32),
            VMEM(grid, f32),
            VMEM((gx * MESSAGE, rows), bf16),
            VMEM((gx * MESSAGE, tile), bf16),
            semaphores(3),
        ],
        flops=1 << 34,
    )
    again = lax.all_to_all(
        message.reshape(senders * MESSAGE // 2, 2, tile), ("sec", "gx"), 0, 0, tiled=True
    )
    (edge_b,) = call(pass_kernel, "pass_edge", [(edge_b, HBM), (carry, HBM), still_a], [edge], aliases={0: 0})
    still_b = swap("gx", 1, edge_b)
    final, mine, index = call(
        second_kernel,
        "second_step",
        [
            (v, HBM)
            for v in (carry, columns, flag, matrices, sea, surface_2d, coefficient, profile, wanted)
        ],
        [((levels, cells), bf16, HBM), ((PLANES, *grid), f32), ((rows, 2), jnp.int32)],
        [
            VMEM(grid, f32),
            VMEM((levels, cells), bf16),
            VMEM((1, cells), bf16),
            VMEM(matrices.shape, bf16),
            VMEM(grid, jnp.int32),
            VMEM(grid, bf16),
            VMEM(wanted.shape, jnp.int32),
            semaphores(6),
            semaphores(PIECES),
        ],
        flops=1 << 34,
    )
    hot, planes = call(
        ready_kernel,
        "ready_import",
        [mine, index, still_a, still_b],
        [((2 * total + 2 * HALO, senders * MESSAGE), bf16), ((PLANES, total, tile), f32)],
    )
    wide, to_a, to_b = call(
        third_kernel,
        "second_import",
        [again.reshape(senders * MESSAGE, tile), weights, hot, planes, still_a, still_b],
        [((PLANES, total, tile), f32), ((total, tile), f32), ((total, tile), f32)],
        [
            VMEM((total, 2 * tile), f32),
            VMEM((total, tile), f32),
        ],
    )
    from_a, from_b = swap("gy", 0, to_a), swap("gy", 1, to_b)
    (surface_out,) = call(
        fourth_kernel,
        "passes",
        [wide, from_a, from_b, (surface_2d, HBM)],
        [(grid, f32)],
        [semaphores(1)],
    )
    return (final.reshape(profile.shape), surface_out.reshape(surface.shape))


def solution(mesh):
    return jax.shard_map(
        body,
        mesh=mesh,
        in_specs=(
            P("sec", None, "gx", "gy"),
            P("sec", "gx", "gy"),
            P("sec", "gx", "gy"),
            P("sec", "gx", "gy"),
            P("sec", "gx", "gy"),
            P("sec", None, None, None),
            P("sec", "gx", "gy", None, None, None, None),
            P("sec", "gx", "gy", None, None),
            P("sec", "gx", "gy", None, None),
        ),
        out_specs=(P("sec", None, "gx", "gy"), P("sec", "gx", "gy")),
        check_vma=False,
    )
```

```python
import functools

import jax
import jax.numpy as jnp
from jax import lax
from jax.experimental import pallas as pl
from jax.experimental.pallas import tpu as pltpu
from jax.sharding import PartitionSpec as P

PHYS = 4
PASSES = 4
HALO = 8
NEAR = 3
PLANES = 5
WIDTH = 2048
PIECES = 8
MESSAGE = 8
bf16 = jnp.bfloat16
f32 = jnp.float32
HBM = pltpu.HBM
VMEM = pltpu.VMEM
VMEM_LIMIT = 16 * 1024 * 1024


def call(kernel, name, operands, outs, scratch=(), flops=0, aliases=None):
    values, specs = [], []
    for operand in operands:
        value, place = operand if isinstance(operand, tuple) else (operand, None)
        if place is not None:
            value = pltpu.with_memory_space_constraint(value, place)
        values.append(value)
        specs.append(pl.BlockSpec(memory_space=HBM if place is HBM else VMEM))
    shapes = [
        out[2](out[0], out[1]) if len(out) > 2 else jax.ShapeDtypeStruct(out[0], out[1]) for out in outs
    ]
    return pl.pallas_call(
        kernel,
        out_shape=shapes,
        in_specs=specs,
        out_specs=[pl.BlockSpec(memory_space=out[2] if len(out) > 2 else VMEM) for out in outs],
        scratch_shapes=list(scratch),
        input_output_aliases=aliases or {},
        name=name,
        cost_estimate=pl.CostEstimate(flops=flops, bytes_accessed=1 << 20, transcendentals=0),
        compiler_params=pltpu.CompilerParams(vmem_limit_bytes=VMEM_LIMIT),
    )(*values)


def fetch(sems, *pairs):
    copies = [pltpu.make_async_copy(source, target, sems.at[n]) for n, (source, target) in enumerate(pairs)]
    for copy in copies:
        copy.start()
    return copies


def pieces(source, target):
    size = source.shape[0] // PIECES
    return [(source.at[n * size : (n + 1) * size], target.at[n * size : (n + 1) * size]) for n in range(PIECES)]


def is_ocean():
    return lax.axis_index("sec") == lax.axis_size("sec") - 1


def is_even(axis):
    return lax.rem(lax.axis_index(axis), 2) == 0


def next_first():
    return jnp.logical_not(is_even("gx"))


def iota(shape, dim):
    return lax.broadcasted_iota(jnp.int32, shape, dim)


def one_hot(flags):
    return jnp.where(flags, 1.0, 0.0).astype(bf16)


def spread(rows, column, odd):
    hot = one_hot(iota((column.shape[0], rows.shape[1]), 1) == column)
    values = rows.astype(f32).astype(bf16)
    both = lax.dot_general(hot, values, (((1,), (1,)), ((), ())), preferred_element_type=f32)
    return jnp.where(odd == 1, both[:, 1:2], both[:, 0:1]).astype(jnp.int32)


def upright(rows, first=0, count=None):
    count = rows.shape[1] if count is None else count
    unit = one_hot(iota((count, rows.shape[1]), 0) + first == iota((count, rows.shape[1]), 1))
    values = rows.astype(f32).astype(bf16)
    turned = lax.dot_general(unit, values, (((1,), (1,)), ((), ())), preferred_element_type=f32)
    return turned.astype(jnp.int32)


def select_kernel(profile, lists_ref, out_ref, lowest, tiles_v, lists_v, sems):
    copies = fetch(sems, (lists_ref, lists_v), (profile.at[0, 0], tiles_v))
    row = iota((out_ref.shape[0], 1), 0)
    copies[0].wait()
    tile = spread(lists_v[...], row >> 1, row & 1)
    hot = one_hot(iota((out_ref.shape[0], tiles_v.shape[0]), 1) == tile)
    copies[1].wait()
    tiles = tiles_v[...]
    out_ref[...] = jnp.dot(hot, tiles, preferred_element_type=f32).astype(bf16)
    lowest[...] = tiles.astype(f32)


def parts(values):
    high = values.astype(bf16).astype(f32)
    rest = values - high
    middle = rest.astype(bf16).astype(f32)
    return [high, middle, rest - middle]


def edges_kernel(
    surface, diffusion, sea, profile, sources, weights, lists, to_a, to_b, hot, hot_message,
    surface_v, diffusion_v, sea_v, level_v, sources_v, lists_v, edge_v, hot_v, sems,
):
    rows, size = surface_v.shape
    count = 2 * NEAR
    last = next_first()
    near = jnp.where(last, 2 * rows - count, 0)
    pairs = (
        (weights.at[pl.ds(near, count)], edge_v.at[0, 0:count]),
        (weights.at[pl.ds(2 * rows - count - near, count)], edge_v.at[1, 0:count]),
        (surface, surface_v),
        (diffusion, diffusion_v),
        (sea, sea_v),
        (profile.at[0, 0], level_v),
        (sources, sources_v),
        (lists, lists_v),
    )
    copies = [pltpu.make_async_copy(source, target, sems.at[n]) for n, (source, target) in enumerate(pairs)]
    copies[-2].start()
    copies[-1].start()

    @pl.when(is_ocean())
    def _():
        for copy in copies[:-2]:
            copy.start()

    row = iota((hot_v.shape[0], 1), 0)
    target, m = (row >> 3) + lists_v.shape[1] - lax.axis_size("gx"), row & 7
    own = lax.axis_index("sec") * lax.axis_size("gx") + lax.axis_index("gx")
    of_edge = jnp.where(target == own + 1, rows - HALO + m, jnp.where(target == own - 1, m, -1))
    copies[-2].wait()
    copies[-1].wait()
    of_tiles = spread(lists_v[...], target - 1 + (m >> 1), m & 1)
    wanted = jnp.where(is_ocean(), of_edge, of_tiles)
    hot_v[...] = one_hot(iota(hot_v.shape, 1) == wanted)
    sent = pltpu.make_async_copy(hot_v, hot_message, sems.at[len(copies)])
    sent.start()
    q = upright(sources_v[...])
    place = iota((rows, hot.shape[1]), 1)
    hot[...] = jnp.concatenate([one_hot(q[:, k : k + 1] == place) for k in (0, 1)], axis=0)

    @pl.when(is_ocean())
    def _():
        for copy in copies[2:-2]:
            copy.wait()
        held = jnp.concatenate([sources_v[...].astype(f32), jnp.zeros((2, size - rows), f32)], axis=1)
        fields = (
            *parts(surface_v[...]),
            *parts(diffusion_v[...]),
            sea_v[...].astype(f32),
            level_v[...].astype(f32),
        )
        for n in (0, 1):
            tail = last if n == 0 else jnp.logical_not(last)
            pieces = [jnp.where(tail, v[rows - HALO : rows], v[0:HALO]) for v in fields] + [held]
            used = sum(piece.shape[0] for piece in pieces)
            pieces.append(jnp.zeros((size - used, size), f32))
            edge_v[n, count] = jnp.concatenate(pieces, axis=0).astype(bf16)
        copies[0].wait()
        copies[1].wait()
        for copy in fetch(sems, (edge_v.at[0], to_a), (edge_v.at[1], to_b)):
            copy.wait()

    sent.wait()


def pass_kernel(edge, *refs):
    pass


def import_group(pick, first, blocks):
    rows = pick[first : first + 8, :].astype(bf16)
    size = pick.shape[1] // 2
    place = iota((8, size), 0)
    held = sorted(blocks)
    made = jnp.zeros((8, size), f32)
    for at in range(0, len(held), 2):
        pair = held[at : at + 2]
        block = jnp.concatenate([jnp.concatenate(blocks[n], axis=1) for n in pair], axis=0)
        found = lax.dot_general(rows, block, (((1,), (1,)), ((), ())), preferred_element_type=f32)
        for m, n in enumerate(pair):
            made = jnp.where(place == n, found[:, m * size : (m + 1) * size], made)
    return made


def import_rows(pick, weights, out, rows):
    for first in range(0, rows, 8):
        blocks = {n: (weights[2 * (first + n)], weights[2 * (first + n) + 1]) for n in range(8)}
        out[first : first + 8] = import_group(pick, first, blocks)


def substep(x, flag, mix):
    deep = x * flag
    both = jnp.concatenate([x - deep, deep], axis=0)
    mixed = jnp.dot(mix, both, preferred_element_type=f32)
    return (0.5 * x.astype(f32) + jnp.tanh(mixed)).astype(bf16)


def with_bottom(x, bottom):
    top = x[0:16].astype(f32)
    top = jnp.where(iota(top.shape, 0) == 0, bottom, top).astype(bf16)
    return jnp.concatenate([top, x[16:]], axis=0)


def flat_rows(grid, first, count):
    return jnp.concatenate([grid[first + r : first + r + 1] for r in range(count)], axis=1)


def first_kernel(
    received, hot, weights, lowest_ref, sea, x_ref, flag_ref, mixing, hot_message,
    message, carry, pick, low_f, carry_v, hot_v, message_v, sems,
):
    rows, tile = carry_v.shape
    pltpu.make_async_copy(hot_message, hot_v, sems.at[1]).start()
    picked = jnp.dot(hot[...], received[...], preferred_element_type=f32)
    pick[:, 0:tile] = picked[0:rows]
    pick[:, tile : 2 * tile] = picked[rows : 2 * rows]
    import_rows(pick, weights, carry_v, rows)
    lowest = lowest_ref[...]
    flux = sea[...].astype(f32) * (carry_v[...] - lowest)
    kept = pltpu.make_async_copy(carry_v, carry, sems.at[0])

    def send(rows_of):
        pltpu.make_async_copy(hot_message, hot_v, sems.at[1]).wait()
        made = jnp.dot(hot_v[...], rows_of.astype(bf16), preferred_element_type=f32)
        message_v[...] = made.astype(bf16)
        total, count = message.shape[0], message_v.shape[0]
        (copy,) = fetch(sems.at[2:3], (message_v, message.at[total - count : total]))
        copy.wait()

    @pl.when(is_ocean())
    def _():
        forcing = flux * (1.0 / PASSES)
        carry_v[...] = forcing
        kept.start()
        send(forcing)

    @pl.when(jnp.logical_not(is_ocean()))
    def _():
        kept.start()
        mix = jnp.concatenate([mixing[0], mixing[1]], axis=1)
        bottom = (lowest + flux).astype(bf16).astype(f32)
        per = WIDTH // tile
        for c in range(x_ref.shape[1] // WIDTH):
            cols = slice(c * WIDTH, (c + 1) * WIDTH)
            flag = flag_ref[:, cols]
            x = with_bottom(x_ref[:, cols], flat_rows(bottom, c * per, per))
            for _ in range(PHYS - 1):
                x = substep(x, flag, mix)
            deep = x * flag
            both = jnp.concatenate([x - deep, deep], axis=0)
            mixed = jnp.dot(mix[0:16], both, preferred_element_type=f32)
            last = 0.5 * x[0:16].astype(f32) + jnp.tanh(mixed)
            for r in range(per):
                low_f[c * per + r : c * per + r + 1, :] = last[0:1, r * tile : (r + 1) * tile]
        send(low_f[...])

    kept.wait()


def second_kernel(
    carry, x_ref, flag_ref, mixing, sea, surface, diffusion, profile, sources,
    out, mine, index,
    carry_v, x_v, flag_v, mixing_v, sea_v, level_v, sources_v, sems, x_sems,
):
    @pl.when(is_ocean())
    def _():
        held = fetch(x_sems, *pieces(x_ref, x_v))
        copies = fetch(
            sems,
            (surface, mine.at[0]),
            (diffusion, mine.at[1]),
            (carry, mine.at[4]),
            (sea, sea_v),
            (profile.at[0, 0], level_v),
            (sources, sources_v),
        )
        for copy in copies:
            copy.wait()
        mine[2] = sea_v[...].astype(f32)
        mine[3] = level_v[...].astype(f32)
        q = upright(sources_v[...])
        index[...] = (q >> 1) * MESSAGE + (q & 1) + 2
        for copy in held:
            copy.wait()
        for copy in fetch(x_sems, *pieces(x_v, out)):
            copy.wait()

    @pl.when(jnp.logical_not(is_ocean()))
    def _():
        pairs = ((carry, carry_v), (sea, sea_v), (mixing, mixing_v), (flag_ref, flag_v))
        for copy in fetch(sems, *pairs) + fetch(x_sems, *pieces(x_ref, x_v)):
            copy.wait()
        mix = jnp.concatenate([mixing_v[0], mixing_v[1]], axis=1)
        sea_f = sea_v[...].astype(f32)
        imported = carry_v[...]
        per = WIDTH // carry_v.shape[1]
        for c in range(x_v.shape[1] // WIDTH):
            cols = slice(c * WIDTH, (c + 1) * WIDTH)
            flag = flag_v[:, cols]
            x = x_v[:, cols]
            wet = flat_rows(sea_f, c * per, per)
            brought = flat_rows(imported, c * per, per)
            for _ in range(2):
                low = x[0:16].astype(f32)[0:1]
                x = with_bottom(x, (low + wet * (brought - low)).astype(bf16).astype(f32))
                for _ in range(PHYS):
                    x = substep(x, flag, mix)
            x_v[:, cols] = x
        for copy in fetch(x_sems, *pieces(x_v, out)):
            copy.wait()


def ready_kernel(mine, own_index, still_a, still_b, hot, planes):
    @pl.when(is_ocean())
    def _():
        rows, tile = mine.shape[1:]
        total = rows + 2 * HALO
        even = next_first()
        edges = [still[2 * NEAR].astype(f32) for still in (still_a, still_b)]
        below = jnp.where(even, edges[0], edges[1])
        above = jnp.where(even, edges[1], edges[0])

        def whole_of(values, at, pieces):
            held = [below[at : at + HALO], above[at : at + HALO]]
            for n in range(1, pieces):
                part = slice(at + n * HALO, at + (n + 1) * HALO)
                held = [held[0] + below[part], held[1] + above[part]]
            return jnp.concatenate([values, *held], axis=0)

        planes[0] = whole_of(mine[0], 0, 3)
        planes[1] = whole_of(mine[1], 3 * HALO, 3)
        planes[2] = whole_of(mine[2], 6 * HALO, 1)
        planes[3] = whole_of(mine[3], 7 * HALO, 1)
        planes[4, 0:rows] = mine[4]
        planes[4, rows:total] = jnp.zeros((2 * HALO, tile), f32)

        at = slice(8 * HALO, 8 * HALO + 2)
        held = [own_index[...]]
        for edge, first, offset in ((below, 0, 4), (above, rows - HALO, 0)):
            q = upright(edge[at, 0:rows].astype(jnp.int32), first, HALO)
            held.append((q >> 1) * MESSAGE + (q & 1) + offset)
        q = jnp.concatenate(held, axis=0)
        place = iota((total, hot.shape[1]), 1)
        own = lax.axis_index("sec") * lax.axis_size("gx") + lax.axis_index("gx")
        row = iota((2 * HALO, 1), 0)
        beyond = jnp.where(row < HALO, (own + 1) * MESSAGE, (own - 1) * MESSAGE - HALO) + row
        place_b = iota((2 * HALO, hot.shape[1]), 1)
        hot[...] = jnp.concatenate(
            [one_hot(q[:, 0:1] == place), one_hot(q[:, 1:2] == place), one_hot(beyond == place_b)], axis=0
        )


def third_kernel(
    received, weights, hot, planes, still_a, still_b, wide, to_a, to_b, pick, imported
):
    @pl.when(is_ocean())
    def _():
        total, tile = imported.shape
        rows = total - 2 * HALO
        picked = jnp.dot(hot[...], received[...], preferred_element_type=f32)
        pick[:, 0:tile] = picked[0:total]
        pick[:, tile : 2 * tile] = picked[total : 2 * total]
        import_rows(pick, weights, imported, rows)
        below_first = next_first()
        for start, last, pair in (
            (rows, False, (still_a, still_b)),
            (rows + HALO, True, (still_b, still_a)),
        ):
            blocks = {}
            for n in range(NEAR):
                block = [jnp.where(below_first, pair[0][2 * n + k], pair[1][2 * n + k]) for k in range(2)]
                blocks[HALO - NEAR + n if last else n] = block
            imported[start : start + HALO] = import_group(pick, start, blocks)
        fields = [
            jnp.concatenate([planes[4, 0:rows], picked[2 * total :]], axis=0),
            planes[2] * (imported[...] - planes[3]) * (1.0 / PASSES),
            planes[0],
            planes[1],
            planes[2],
        ]
        group = iota((total, tile), 1) >> 3
        right = left = fields[0]
        for p, values in enumerate(fields):
            wide[p] = values
            if p:
                right = jnp.where(group == tile // HALO - 1 - p, pltpu.roll(values, tile - HALO * p, 1), right)
                left = jnp.where(group == p, pltpu.roll(values, HALO * p, 1), left)
        even = is_even("gy")
        to_a[...] = jnp.where(even, right, left)
        to_b[...] = jnp.where(even, left, right)


def fourth_kernel(wide, from_a, from_b, surface, out, sems):
    @pl.when(jnp.logical_not(is_ocean()))
    def _():
        fetch(sems, (surface, out))[0].wait()

    @pl.when(is_ocean())
    def _():
        rows, tile = out.shape
        total = wide.shape[1]
        group = iota((total, tile), 1) >> 3
        even = is_even("gy")
        from_right = jnp.where(even, from_a[...], from_b[...])
        from_left = jnp.where(even, from_b[...], from_a[...])
        fields = []
        for p in range(PLANES):
            right, left = from_right, from_left
            if p:
                right = pltpu.roll(right, tile - HALO * p, 1)
                left = pltpu.roll(left, HALO * p, 1)
            beside = jnp.where(group == 0, right, jnp.where(group == tile // HALO - 1, left, 0.0))
            fields.append(jnp.concatenate([wide[p], beside], axis=1))
        forcing_1, forcing_2, height, coefficient, sea = fields
        for forcing in (forcing_1, forcing_2):
            for sweep in range(PASSES):
                around = pltpu.roll(height, total - 1, 0) + pltpu.roll(height, 1, 0)
                around = around + pltpu.roll(height, 2 * tile - 1, 1) + pltpu.roll(height, 1, 1)
                height = sea * (height + coefficient * (around - 4.0 * height) + forcing)
        out[...] = height[0:rows, 0:tile]


def body(
    profile, surface, diffusion, sea_mask, convective, mixing, remap_weights, sources, send_lists
):
    levels, rows, tile = profile.shape[1:]
    cells = rows * tile
    surface_2d = surface.reshape(rows, tile)
    coefficient = diffusion.reshape(rows, tile)
    sea = sea_mask.reshape(rows, tile)
    matrices = mixing.reshape(2, levels, levels)
    weights = remap_weights.reshape(2 * rows, tile, tile)
    wanted = sources.reshape(sources.shape[3:]).T
    lists = send_lists.reshape(send_lists.shape[3:]).T
    slots, senders = lists.shape
    secs = lax.axis_size("sec")
    gx = lax.axis_size("gx")
    gy = lax.axis_size("gy")
    total = rows + 2 * HALO
    grid = (rows, tile)

    base = {"gx": (secs - 1) * gx, "gy": (secs - 1) * gy}
    counts = {"gx": gx, "gy": gy}

    def swap(axis, start, values):
        first = base[axis]
        pairs = [(first + i, first + i + 1) for i in range(start, counts[axis] - 1, 2)]
        return lax.ppermute(values, ("sec", axis), pairs + [(t, s) for s, t in pairs])

    def semaphores(count):
        return pltpu.SemaphoreType.DMA((count,))

    chosen, lowest = call(
        select_kernel,
        "select_tiles",
        [(profile, HBM), (lists, HBM)],
        [((senders * slots, tile), bf16), (grid, f32)],
        [VMEM(grid, bf16), VMEM(lists.shape, jnp.int32), semaphores(2)],
    )
    received = lax.all_to_all(chosen.reshape(senders, slots, tile), ("sec", "gx"), 0, 0, tiled=True)

    edge = ((2 * NEAR + 1, tile, tile), bf16, HBM)
    edge_operands = [(v, HBM) for v in (surface_2d, coefficient, sea, profile, wanted, weights)]
    edge_scratch = [
        VMEM(grid, f32),
        VMEM(grid, f32),
        VMEM(grid, jnp.int32),
        VMEM(grid, bf16),
        VMEM(wanted.shape, jnp.int32),
    ]
    edge_a, edge_b, hot_first, hot_message = call(
        edges_kernel,
        "edge_rows",
        [*edge_operands, (lists, HBM)],
        [edge, edge, ((2 * rows, senders * slots), bf16), ((gx * MESSAGE, rows), bf16, HBM)],
        [
            *edge_scratch,
            VMEM(lists.shape, jnp.int32),
            VMEM((2, *edge[0]), bf16),
            VMEM((gx * MESSAGE, rows), bf16),
            semaphores(9),
        ],
    )
    still_a = swap("gx", 1, edge_a)

    columns = profile.reshape(levels, cells)
    flag = convective.reshape(1, cells).astype(bf16)
    message, carry = call(
        first_kernel,
        "first_step",
        [
            received.reshape(senders * slots, tile), hot_first, weights, lowest, sea, (columns, VMEM),
            flag, matrices, (hot_message, HBM),
        ],
        [((senders * MESSAGE, tile), bf16, HBM), (grid, f32, HBM)],
        [
            VMEM((rows, 2 * tile), f32),
            VMEM(grid, f32),
            VMEM(grid, f32),
            VMEM((gx * MESSAGE, rows), bf16),
            VMEM((gx * MESSAGE, tile), bf16),
            semaphores(3),
        ],
        flops=1 << 34,
    )
    again = lax.all_to_all(
        message.reshape(senders * MESSAGE // 2, 2, tile), ("sec", "gx"), 0, 0, tiled=True
    )
    (edge_b,) = call(pass_kernel, "pass_edge", [(edge_b, HBM), (carry, HBM), still_a], [edge], aliases={0: 0})
    still_b = swap("gx", 0, edge_b)
    final, mine, index = call(
        second_kernel,
        "second_step",
        [
            (v, HBM)
            for v in (carry, columns, flag, matrices, sea, surface_2d, coefficient, profile, wanted)
        ],
        [((levels, cells), bf16, HBM), ((PLANES, *grid), f32), ((rows, 2), jnp.int32)],
        [
            VMEM(grid, f32),
            VMEM((levels, cells), bf16),
            VMEM((1, cells), bf16),
            VMEM(matrices.shape, bf16),
            VMEM(grid, jnp.int32),
            VMEM(grid, bf16),
            VMEM(wanted.shape, jnp.int32),
            semaphores(6),
            semaphores(PIECES),
        ],
        flops=1 << 34,
    )
    hot, planes = call(
        ready_kernel,
        "ready_import",
        [mine, index, still_a, still_b],
        [((2 * total + 2 * HALO, senders * MESSAGE), bf16), ((PLANES, total, tile), f32)],
    )
    wide, to_a, to_b = call(
        third_kernel,
        "second_import",
        [again.reshape(senders * MESSAGE, tile), weights, hot, planes, still_a, still_b],
        [((PLANES, total, tile), f32), ((total, tile), f32), ((total, tile), f32)],
        [
            VMEM((total, 2 * tile), f32),
            VMEM((total, tile), f32),
        ],
    )
    from_a, from_b = swap("gy", 0, to_a), swap("gy", 1, to_b)
    (surface_out,) = call(
        fourth_kernel,
        "passes",
        [wide, from_a, from_b, (surface_2d, HBM)],
        [(grid, f32)],
        [semaphores(1)],
    )
    return (final.reshape(profile.shape), surface_out.reshape(surface.shape))


def solution(mesh):
    return jax.shard_map(
        body,
        mesh=mesh,
        in_specs=(
            P("sec", None, "gx", "gy"),
            P("sec", "gx", "gy"),
            P("sec", "gx", "gy"),
            P("sec", "gx", "gy"),
            P("sec", "gx", "gy"),
            P("sec", None, None, None),
            P("sec", "gx", "gy", None, None, None, None),
            P("sec", "gx", "gy", None, None),
            P("sec", "gx", "gy", None, None),
        ),
        out_specs=(P("sec", None, "gx", "gy"), P("sec", "gx", "gy")),
        check_vma=False,
    )
```

```python
import functools

import jax
import jax.numpy as jnp
from jax import lax
from jax.experimental import pallas as pl
from jax.experimental.pallas import tpu as pltpu
from jax.sharding import PartitionSpec as P

PHYS = 4
PASSES = 4
HALO = 8
NEAR = 3
PLANES = 5
WIDTH = 2048
PIECES = 8
MESSAGE = 8
bf16 = jnp.bfloat16
f32 = jnp.float32
HBM = pltpu.HBM
VMEM = pltpu.VMEM
VMEM_LIMIT = 16 * 1024 * 1024


def call(kernel, name, operands, outs, scratch=(), flops=0, aliases=None):
    values, specs = [], []
    for operand in operands:
        value, place = operand if isinstance(operand, tuple) else (operand, None)
        if place is not None:
            value = pltpu.with_memory_space_constraint(value, place)
        values.append(value)
        specs.append(pl.BlockSpec(memory_space=HBM if place is HBM else VMEM))
    shapes = [
        out[2](out[0], out[1]) if len(out) > 2 else jax.ShapeDtypeStruct(out[0], out[1]) for out in outs
    ]
    return pl.pallas_call(
        kernel,
        out_shape=shapes,
        in_specs=specs,
        out_specs=[pl.BlockSpec(memory_space=out[2] if len(out) > 2 else VMEM) for out in outs],
        scratch_shapes=list(scratch),
        input_output_aliases=aliases or {},
        name=name,
        cost_estimate=pl.CostEstimate(flops=flops, bytes_accessed=1 << 20, transcendentals=0),
        compiler_params=pltpu.CompilerParams(vmem_limit_bytes=VMEM_LIMIT),
    )(*values)


def fetch(sems, *pairs):
    copies = [pltpu.make_async_copy(source, target, sems.at[n]) for n, (source, target) in enumerate(pairs)]
    for copy in copies:
        copy.start()
    return copies


def pieces(source, target):
    size = source.shape[0] // PIECES
    return [(source.at[n * size : (n + 1) * size], target.at[n * size : (n + 1) * size]) for n in range(PIECES)]


def is_ocean():
    return lax.axis_index("sec") == lax.axis_size("sec") - 1


def is_even(axis):
    return lax.rem(lax.axis_index(axis), 2) == 0


def next_first():
    return jnp.logical_not(is_even("gx"))


def iota(shape, dim):
    return lax.broadcasted_iota(jnp.int32, shape, dim)


def one_hot(flags):
    return jnp.where(flags, 1.0, 0.0).astype(bf16)


def spread(rows, column, odd):
    hot = one_hot(iota((column.shape[0], rows.shape[1]), 1) == column)
    values = rows.astype(f32).astype(bf16)
    both = lax.dot_general(hot, values, (((1,), (1,)), ((), ())), preferred_element_type=f32)
    return jnp.where(odd == 1, both[:, 1:2], both[:, 0:1]).astype(jnp.int32)


def upright(rows, first=0, count=None):
    count = rows.shape[1] if count is None else count
    unit = one_hot(iota((count, rows.shape[1]), 0) + first == iota((count, rows.shape[1]), 1))
    values = rows.astype(f32).astype(bf16)
    turned = lax.dot_general(unit, values, (((1,), (1,)), ((), ())), preferred_element_type=f32)
    return turned.astype(jnp.int32)


def select_kernel(profile, lists_ref, out_ref, lowest, tiles_v, lists_v, sems):
    copies = fetch(sems, (lists_ref, lists_v), (profile.at[0, 0], tiles_v))
    row = iota((out_ref.shape[0], 1), 0)
    copies[0].wait()
    tile = spread(lists_v[...], row >> 1, row & 1)
    hot = one_hot(iota((out_ref.shape[0], tiles_v.shape[0]), 1) == tile)
    copies[1].wait()
    tiles = tiles_v[...]
    out_ref[...] = jnp.dot(hot, tiles, preferred_element_type=f32).astype(bf16)
    lowest[...] = tiles.astype(f32)


def parts(values):
    high = values.astype(bf16).astype(f32)
    rest = values - high
    middle = rest.astype(bf16).astype(f32)
    return [high, middle, rest - middle]


def edges_kernel(
    surface, diffusion, sea, profile, sources, weights, lists, to_a, to_b, hot, hot_message,
    surface_v, diffusion_v, sea_v, level_v, sources_v, lists_v, edge_v, hot_v, sems,
):
    rows, size = surface_v.shape
    count = 2 * NEAR
    last = next_first()
    near = jnp.where(last, 2 * rows - count, 0)
    pairs = (
        (weights.at[pl.ds(near, count)], edge_v.at[0, 0:count]),
        (weights.at[pl.ds(2 * rows - count - near, count)], edge_v.at[1, 0:count]),
        (surface, surface_v),
        (diffusion, diffusion_v),
        (sea, sea_v),
        (profile.at[0, 0], level_v),
        (sources, sources_v),
        (lists, lists_v),
    )
    copies = [pltpu.make_async_copy(source, target, sems.at[n]) for n, (source, target) in enumerate(pairs)]
    copies[-2].start()
    copies[-1].start()

    @pl.when(is_ocean())
    def _():
        for copy in copies[:-2]:
            copy.start()

    row = iota((hot_v.shape[0], 1), 0)
    target, m = (row >> 3) + lists_v.shape[1] - lax.axis_size("gx"), row & 7
    own = lax.axis_index("sec") * lax.axis_size("gx") + lax.axis_index("gx")
    of_edge = jnp.where(target == own + 1, rows - HALO + m, jnp.where(target == own - 1, m, -1))
    copies[-2].wait()
    copies[-1].wait()
    of_tiles = spread(lists_v[...], target - 1 + (m >> 1), m & 1)
    wanted = jnp.where(is_ocean(), of_edge, of_tiles)
    hot_v[...] = one_hot(iota(hot_v.shape, 1) == wanted)
    sent = pltpu.make_async_copy(hot_v, hot_message, sems.at[len(copies)])
    sent.start()
    q = upright(sources_v[...])
    place = iota((rows, hot.shape[1]), 1)
    hot[...] = jnp.concatenate([one_hot(q[:, k : k + 1] == place) for k in (0, 1)], axis=0)

    @pl.when(is_ocean())
    def _():
        for copy in copies[2:-2]:
            copy.wait()
        held = jnp.concatenate([sources_v[...].astype(f32), jnp.zeros((2, size - rows), f32)], axis=1)
        fields = (
            *parts(surface_v[...]),
            *parts(diffusion_v[...]),
            sea_v[...].astype(f32),
            level_v[...].astype(f32),
        )
        for n in (0, 1):
            tail = last if n == 0 else jnp.logical_not(last)
            pieces = [jnp.where(tail, v[rows - HALO : rows], v[0:HALO]) for v in fields] + [held]
            used = sum(piece.shape[0] for piece in pieces)
            pieces.append(jnp.zeros((size - used, size), f32))
            edge_v[n, count] = jnp.concatenate(pieces, axis=0).astype(bf16)
        copies[0].wait()
        copies[1].wait()
        for copy in fetch(sems, (edge_v.at[0], to_a), (edge_v.at[1], to_b)):
            copy.wait()

    sent.wait()


def pass_kernel(edge, *refs):
    pass


def import_group(pick, first, blocks):
    rows = pick[first : first + 8, :].astype(bf16)
    size = pick.shape[1] // 2
    place = iota((8, size), 0)
    held = sorted(blocks)
    made = jnp.zeros((8, size), f32)
    for at in range(0, len(held), 2):
        pair = held[at : at + 2]
        block = jnp.concatenate([jnp.concatenate(blocks[n], axis=1) for n in pair], axis=0)
        found = lax.dot_general(rows, block, (((1,), (1,)), ((), ())), preferred_element_type=f32)
        for m, n in enumerate(pair):
            made = jnp.where(place == n, found[:, m * size : (m + 1) * size], made)
    return made


def import_rows(pick, weights, out, first, count):
    made = []
    for at in range(first, first + count, 8):
        blocks = {n: (weights[2 * (at + n)], weights[2 * (at + n) + 1]) for n in range(8)}
        made.append(import_group(pick, at, blocks))
        out[at : at + 8] = made[-1]
    return jnp.concatenate(made, axis=0)


def substep(x, flag, mix):
    deep = x * flag
    both = jnp.concatenate([x - deep, deep], axis=0)
    mixed = jnp.dot(mix, both, preferred_element_type=f32)
    return (0.5 * x.astype(f32) + jnp.tanh(mixed)).astype(bf16)


def with_bottom(x, bottom):
    top = x[0:16].astype(f32)
    top = jnp.where(iota(top.shape, 0) == 0, bottom, top).astype(bf16)
    return jnp.concatenate([top, x[16:]], axis=0)


def flat_rows(grid, first, count):
    return jnp.concatenate([grid[first + r : first + r + 1] for r in range(count)], axis=1)


def first_kernel(
    received, hot, weights, lowest_ref, sea, x_ref, flag_ref, mixing, hot_message,
    message, carry, pick, low_f, carry_v, hot_v, message_v, sems,
):
    rows, tile = carry_v.shape
    pltpu.make_async_copy(hot_message, hot_v, sems.at[1]).start()
    picked = jnp.dot(hot[...], received[...], preferred_element_type=f32)
    pick[:, 0:tile] = picked[0:rows]
    pick[:, tile : 2 * tile] = picked[rows : 2 * rows]
    lowest = lowest_ref[...]
    sea_f = sea[...].astype(f32)
    kept = pltpu.make_async_copy(carry_v, carry, sems.at[0])

    def send(rows_of):
        pltpu.make_async_copy(hot_message, hot_v, sems.at[1]).wait()
        made = jnp.dot(hot_v[...], rows_of.astype(bf16), preferred_element_type=f32)
        message_v[...] = made.astype(bf16)
        total, count = message.shape[0], message_v.shape[0]
        (copy,) = fetch(sems.at[2:3], (message_v, message.at[total - count : total]))
        copy.wait()

    @pl.when(is_ocean())
    def _():
        imported = import_rows(pick, weights, carry_v, 0, rows)
        forcing = sea_f * (imported - lowest) * (1.0 / PASSES)
        carry_v[...] = forcing
        kept.start()
        send(forcing)

    @pl.when(jnp.logical_not(is_ocean()))
    def _():
        mix = jnp.concatenate([mixing[0], mixing[1]], axis=1)
        per = WIDTH // tile
        for c in range(x_ref.shape[1] // WIDTH):
            cols = slice(c * WIDTH, (c + 1) * WIDTH)
            part = slice(c * per, (c + 1) * per)
            flag = flag_ref[:, cols]
            flux = sea_f[part] * (import_rows(pick, weights, carry_v, c * per, per) - lowest[part])
            bottom = (lowest[part] + flux).astype(bf16).astype(f32)
            x = with_bottom(x_ref[:, cols], flat_rows(bottom, 0, per))
            for _ in range(PHYS - 1):
                x = substep(x, flag, mix)
            deep = x * flag
            both = jnp.concatenate([x - deep, deep], axis=0)
            mixed = jnp.dot(mix[0:16], both, preferred_element_type=f32)
            last = 0.5 * x[0:16].astype(f32) + jnp.tanh(mixed)
            for r in range(per):
                low_f[c * per + r : c * per + r + 1, :] = last[0:1, r * tile : (r + 1) * tile]
        kept.start()
        send(low_f[...])

    kept.wait()


def second_kernel(
    carry, x_ref, flag_ref, mixing, sea, surface, diffusion, profile, sources,
    out, mine, index,
    carry_v, x_v, flag_v, mixing_v, sea_v, level_v, sources_v, sems, x_sems,
):
    @pl.when(is_ocean())
    def _():
        held = fetch(x_sems, *pieces(x_ref, x_v))
        copies = fetch(
            sems,
            (surface, mine.at[0]),
            (diffusion, mine.at[1]),
            (carry, mine.at[4]),
            (sea, sea_v),
            (profile.at[0, 0], level_v),
            (sources, sources_v),
        )
        for copy in copies:
            copy.wait()
        mine[2] = sea_v[...].astype(f32)
        mine[3] = level_v[...].astype(f32)
        q = upright(sources_v[...])
        index[...] = (q >> 1) * MESSAGE + (q & 1) + 2
        for copy in held:
            copy.wait()
        for copy in fetch(x_sems, *pieces(x_v, out)):
            copy.wait()

    @pl.when(jnp.logical_not(is_ocean()))
    def _():
        pairs = ((carry, carry_v), (sea, sea_v), (mixing, mixing_v), (flag_ref, flag_v))
        for copy in fetch(sems, *pairs) + fetch(x_sems, *pieces(x_ref, x_v)):
            copy.wait()
        mix = jnp.concatenate([mixing_v[0], mixing_v[1]], axis=1)
        sea_f = sea_v[...].astype(f32)
        imported = carry_v[...]
        per = WIDTH // carry_v.shape[1]
        for c in range(x_v.shape[1] // WIDTH):
            cols = slice(c * WIDTH, (c + 1) * WIDTH)
            flag = flag_v[:, cols]
            x = x_v[:, cols]
            wet = flat_rows(sea_f, c * per, per)
            brought = flat_rows(imported, c * per, per)
            for _ in range(2):
                low = x[0:16].astype(f32)[0:1]
                x = with_bottom(x, (low + wet * (brought - low)).astype(bf16).astype(f32))
                for _ in range(PHYS):
                    x = substep(x, flag, mix)
            x_v[:, cols] = x
        for copy in fetch(x_sems, *pieces(x_v, out)):
            copy.wait()


def ready_kernel(mine, own_index, still_a, still_b, hot, planes):
    @pl.when(is_ocean())
    def _():
        rows, tile = mine.shape[1:]
        total = rows + 2 * HALO
        even = next_first()
        edges = [still[2 * NEAR].astype(f32) for still in (still_a, still_b)]
        below = jnp.where(even, edges[0], edges[1])
        above = jnp.where(even, edges[1], edges[0])

        def whole_of(values, at, pieces):
            held = [below[at : at + HALO], above[at : at + HALO]]
            for n in range(1, pieces):
                part = slice(at + n * HALO, at + (n + 1) * HALO)
                held = [held[0] + below[part], held[1] + above[part]]
            return jnp.concatenate([values, *held], axis=0)

        planes[0] = whole_of(mine[0], 0, 3)
        planes[1] = whole_of(mine[1], 3 * HALO, 3)
        planes[2] = whole_of(mine[2], 6 * HALO, 1)
        planes[3] = whole_of(mine[3], 7 * HALO, 1)
        planes[4, 0:rows] = mine[4]
        planes[4, rows:total] = jnp.zeros((2 * HALO, tile), f32)

        at = slice(8 * HALO, 8 * HALO + 2)
        held = [own_index[...]]
        for edge, first, offset in ((below, 0, 4), (above, rows - HALO, 0)):
            q = upright(edge[at, 0:rows].astype(jnp.int32), first, HALO)
            held.append((q >> 1) * MESSAGE + (q & 1) + offset)
        q = jnp.concatenate(held, axis=0)
        place = iota((total, hot.shape[1]), 1)
        own = lax.axis_index("sec") * lax.axis_size("gx") + lax.axis_index("gx")
        row = iota((2 * HALO, 1), 0)
        beyond = jnp.where(row < HALO, (own + 1) * MESSAGE, (own - 1) * MESSAGE - HALO) + row
        place_b = iota((2 * HALO, hot.shape[1]), 1)
        hot[...] = jnp.concatenate(
            [one_hot(q[:, 0:1] == place), one_hot(q[:, 1:2] == place), one_hot(beyond == place_b)], axis=0
        )


def third_kernel(
    received, weights, hot, planes, still_a, still_b, wide, to_a, to_b, pick, imported
):
    @pl.when(is_ocean())
    def _():
        total, tile = imported.shape
        rows = total - 2 * HALO
        picked = jnp.dot(hot[...], received[...], preferred_element_type=f32)
        pick[:, 0:tile] = picked[0:total]
        pick[:, tile : 2 * tile] = picked[total : 2 * total]
        import_rows(pick, weights, imported, 0, rows)
        below_first = next_first()
        for start, last, pair in (
            (rows, False, (still_a, still_b)),
            (rows + HALO, True, (still_b, still_a)),
        ):
            blocks = {}
            for n in range(NEAR):
                block = [jnp.where(below_first, pair[0][2 * n + k], pair[1][2 * n + k]) for k in range(2)]
                blocks[HALO - NEAR + n if last else n] = block
            imported[start : start + HALO] = import_group(pick, start, blocks)
        fields = [
            jnp.concatenate([planes[4, 0:rows], picked[2 * total :]], axis=0),
            planes[2] * (imported[...] - planes[3]) * (1.0 / PASSES),
            planes[0],
            planes[1],
            planes[2],
        ]
        group = iota((total, tile), 1) >> 3
        right = left = fields[0]
        for p, values in enumerate(fields):
            wide[p] = values
            if p:
                right = jnp.where(group == tile // HALO - 1 - p, pltpu.roll(values, tile - HALO * p, 1), right)
                left = jnp.where(group == p, pltpu.roll(values, HALO * p, 1), left)
        even = is_even("gy")
        to_a[...] = jnp.where(even, right, left)
        to_b[...] = jnp.where(even, left, right)


def fourth_kernel(wide, from_a, from_b, surface, out, sems):
    @pl.when(jnp.logical_not(is_ocean()))
    def _():
        fetch(sems, (surface, out))[0].wait()

    @pl.when(is_ocean())
    def _():
        rows, tile = out.shape
        total = wide.shape[1]
        group = iota((total, tile), 1) >> 3
        even = is_even("gy")
        from_right = jnp.where(even, from_a[...], from_b[...])
        from_left = jnp.where(even, from_b[...], from_a[...])
        fields = []
        for p in range(PLANES):
            right, left = from_right, from_left
            if p:
                right = pltpu.roll(right, tile - HALO * p, 1)
                left = pltpu.roll(left, HALO * p, 1)
            beside = jnp.where(group == 0, right, jnp.where(group == tile // HALO - 1, left, 0.0))
            fields.append(jnp.concatenate([wide[p], beside], axis=1))
        forcing_1, forcing_2, height, coefficient, sea = fields
        for forcing in (forcing_1, forcing_2):
            for sweep in range(PASSES):
                around = pltpu.roll(height, total - 1, 0) + pltpu.roll(height, 1, 0)
                around = around + pltpu.roll(height, 2 * tile - 1, 1) + pltpu.roll(height, 1, 1)
                height = sea * (height + coefficient * (around - 4.0 * height) + forcing)
        out[...] = height[0:rows, 0:tile]


def body(
    profile, surface, diffusion, sea_mask, convective, mixing, remap_weights, sources, send_lists
):
    levels, rows, tile = profile.shape[1:]
    cells = rows * tile
    surface_2d = surface.reshape(rows, tile)
    coefficient = diffusion.reshape(rows, tile)
    sea = sea_mask.reshape(rows, tile)
    matrices = mixing.reshape(2, levels, levels)
    weights = remap_weights.reshape(2 * rows, tile, tile)
    wanted = sources.reshape(sources.shape[3:]).T
    lists = send_lists.reshape(send_lists.shape[3:]).T
    slots, senders = lists.shape
    secs = lax.axis_size("sec")
    gx = lax.axis_size("gx")
    gy = lax.axis_size("gy")
    total = rows + 2 * HALO
    grid = (rows, tile)

    base = {"gx": (secs - 1) * gx, "gy": (secs - 1) * gy}
    counts = {"gx": gx, "gy": gy}

    def swap(axis, start, values):
        first = base[axis]
        pairs = [(first + i, first + i + 1) for i in range(start, counts[axis] - 1, 2)]
        return lax.ppermute(values, ("sec", axis), pairs + [(t, s) for s, t in pairs])

    def semaphores(count):
        return pltpu.SemaphoreType.DMA((count,))

    chosen, lowest = call(
        select_kernel,
        "select_tiles",
        [(profile, HBM), (lists, HBM)],
        [((senders * slots, tile), bf16), (grid, f32)],
        [VMEM(grid, bf16), VMEM(lists.shape, jnp.int32), semaphores(2)],
    )
    received = lax.all_to_all(chosen.reshape(senders, slots, tile), ("sec", "gx"), 0, 0, tiled=True)

    edge = ((2 * NEAR + 1, tile, tile), bf16, HBM)
    edge_operands = [(v, HBM) for v in (surface_2d, coefficient, sea, profile, wanted, weights)]
    edge_scratch = [
        VMEM(grid, f32),
        VMEM(grid, f32),
        VMEM(grid, jnp.int32),
        VMEM(grid, bf16),
        VMEM(wanted.shape, jnp.int32),
    ]
    edge_a, edge_b, hot_first, hot_message = call(
        edges_kernel,
        "edge_rows",
        [*edge_operands, (lists, HBM)],
        [edge, edge, ((2 * rows, senders * slots), bf16), ((gx * MESSAGE, rows), bf16, HBM)],
        [
            *edge_scratch,
            VMEM(lists.shape, jnp.int32),
            VMEM((2, *edge[0]), bf16),
            VMEM((gx * MESSAGE, rows), bf16),
            semaphores(9),
        ],
    )
    still_a = swap("gx", 1, edge_a)

    columns = profile.reshape(levels, cells)
    flag = convective.reshape(1, cells).astype(bf16)
    message, carry = call(
        first_kernel,
        "first_step",
        [
            received.reshape(senders * slots, tile), hot_first, weights, lowest, sea, (columns, VMEM),
            flag, matrices, (hot_message, HBM),
        ],
        [((senders * MESSAGE, tile), bf16, HBM), (grid, f32, HBM)],
        [
            VMEM((rows, 2 * tile), f32),
            VMEM(grid, f32),
            VMEM(grid, f32),
            VMEM((gx * MESSAGE, rows), bf16),
            VMEM((gx * MESSAGE, tile), bf16),
            semaphores(3),
        ],
        flops=1 << 34,
    )
    again = lax.all_to_all(
        message.reshape(senders * MESSAGE // 2, 2, tile), ("sec", "gx"), 0, 0, tiled=True
    )
    (edge_b,) = call(pass_kernel, "pass_edge", [(edge_b, HBM), (carry, HBM), still_a], [edge], aliases={0: 0})
    still_b = swap("gx", 0, edge_b)
    final, mine, index = call(
        second_kernel,
        "second_step",
        [
            (v, HBM)
            for v in (carry, columns, flag, matrices, sea, surface_2d, coefficient, profile, wanted)
        ],
        [((levels, cells), bf16, HBM), ((PLANES, *grid), f32), ((rows, 2), jnp.int32)],
        [
            VMEM(grid, f32),
            VMEM((levels, cells), bf16),
            VMEM((1, cells), bf16),
            VMEM(matrices.shape, bf16),
            VMEM(grid, jnp.int32),
            VMEM(grid, bf16),
            VMEM(wanted.shape, jnp.int32),
            semaphores(6),
            semaphores(PIECES),
        ],
        flops=1 << 34,
    )
    hot, planes = call(
        ready_kernel,
        "ready_import",
        [mine, index, still_a, still_b],
        [((2 * total + 2 * HALO, senders * MESSAGE), bf16), ((PLANES, total, tile), f32)],
    )
    wide, to_a, to_b = call(
        third_kernel,
        "second_import",
        [again.reshape(senders * MESSAGE, tile), weights, hot, planes, still_a, still_b],
        [((PLANES, total, tile), f32), ((total, tile), f32), ((total, tile), f32)],
        [
            VMEM((total, 2 * tile), f32),
            VMEM((total, tile), f32),
        ],
    )
    from_a, from_b = swap("gy", 0, to_a), swap("gy", 1, to_b)
    (surface_out,) = call(
        fourth_kernel,
        "passes",
        [wide, from_a, from_b, (surface_2d, HBM)],
        [(grid, f32)],
        [semaphores(1)],
    )
    return (final.reshape(profile.shape), surface_out.reshape(surface.shape))


def solution(mesh):
    return jax.shard_map(
        body,
        mesh=mesh,
        in_specs=(
            P("sec", None, "gx", "gy"),
            P("sec", "gx", "gy"),
            P("sec", "gx", "gy"),
            P("sec", "gx", "gy"),
            P("sec", "gx", "gy"),
            P("sec", None, None, None),
            P("sec", "gx", "gy", None, None, None, None),
            P("sec", "gx", "gy", None, None),
            P("sec", "gx", "gy", None, None),
        ),
        out_specs=(P("sec", None, "gx", "gy"), P("sec", "gx", "gy")),
        check_vma=False,
    )
```
